256 devices in a mesh: mem: 8 (over x, core), tile: 32 (over z, y).
Axes of the slice: x: 4, y: 4, z: 8, core: 2. Of those that a mesh axis runs over, the one named last changes fastest.
Arguments:
- prior_sample: bfloat16 [256, 8, 256, 256], P('mem', None, 'tile'), may hold values from -6 to 6
- measured_position: int32 [256, 2, 256], P(('mem', 'tile')), may hold values from 0 to 1023
- measured_tally: int32 [256, 2], P(('mem', 'tile')), may hold values from 1 to 256, as said below
- measured_datum: float32 [256, 2, 256], P(('mem', 'tile')), may hold values from -6 to 6
- measured_noise_spread: bfloat16 [256, 2, 256], P(('mem', 'tile')), may hold values from 0.25 to 4
Outputs:
- analysis: bfloat16 [256, 8, 256, 256], P('mem', None, 'tile')
The draws below stay inside these ranges and needn't reach their ends.
Inputs may be any that keep to these rules, and one draw needn't show every extreme that they name: `measured_tally`: counts are uneven from row to row, and some block in every draw has all 256 slots live.
All inputs are finite; a program needn't handle non-finite values.
Results may differ from the reference program's by a relative error of at most 0.0055.
The reference program's roundings to bfloat16 on the way (of `anomaly`, `ensemble`, `innovation`, `weights`, `weighted` and `mixing`) count: a program that leaves them out, or rounds other values in their place, can miss the bound.
Values may be sent and summed in bfloat16 or wider, within the bound.
No kernel may reach another device: no remote copies, remote signals or barrier semaphores. Data moves between devices by JAX's collectives and lax.ppermute only.
A program may use at most 64 MiB of HBM per device.

```python
import math
import jax
import jax.numpy as jnp
from jax import lax

MEMBER_TOTAL = 256
TILE_WIDTH = 128
VERTICAL_LAYERS = 8
CBLK = 2
OBS = 256
MESH_WIDTH = 256
MESH_HEIGHT = 256


def draw_measured_tally(key, part):
    key = jax.random.fold_in(key, 7)
    key_base, key_coast, key_fill = jax.random.split(key, 3)
    baseline = jax.random.randint(key_base, (MESH_HEIGHT, CBLK), 1, OBS + 1)
    coastal = jax.random.randint(key_coast, (MESH_HEIGHT, 1), 0, 4)
    counts = jnp.clip(baseline * (coastal + 1) // 2, 1, OBS)
    filled_at = jax.random.randint(key_fill, (), 0, MESH_HEIGHT * CBLK)
    counts = counts.reshape(-1).at[filled_at].set(OBS).reshape(MESH_HEIGHT, CBLK)
    return counts.astype(jnp.int32)


def place_ends(array, key, low, largest):
    place = [jax.random.randint(jax.random.fold_in(key, axis), (), 0, length) for axis, length in enumerate(array.shape)]
    longest = array.shape.index(max(array.shape))
    next_to = place[:longest] + [(place[longest] + 1) % array.shape[longest]] + place[longest + 1:]
    return array.at[tuple(place)].set(low).at[tuple(next_to)].set(largest)


def levels(rng, shape, pieces, low, largest):
    gain = 1.0
    for axis_at, shards_of in pieces:
        heights = jax.random.uniform(jax.random.fold_in(jax.random.fold_in(rng, 6), axis_at), (shards_of,), jnp.float32, low / len(pieces), largest / len(pieces))
        gain = gain * jnp.repeat(jnp.exp(heights), shape[axis_at] // shards_of).reshape((-1,) + (1,) * (len(shape) - 1 - axis_at))
    return gain


def centred(stream_key, shape, deviation, bound, shards=(), kind=jnp.bfloat16):
    level = levels(stream_key, shape, shards, -0.22, 0.18) if shards else 1.0
    drawn = jax.random.normal(stream_key, shape, jnp.float32) * deviation * level
    return jnp.minimum(jnp.maximum(drawn, -bound), bound).astype(kind)


def setup_inputs(seed: int = 0) -> dict:
    arg_keys = jax.random.split(jax.random.key(seed), 6)
    prior_sample = centred(arg_keys[0], (MEMBER_TOTAL, VERTICAL_LAYERS, MESH_WIDTH, MESH_HEIGHT), 1.0, 6.0, ((0, 8), (2, 32)))
    measured_position = place_ends(jax.random.randint(arg_keys[1], (MESH_HEIGHT, CBLK, OBS), 0, VERTICAL_LAYERS * TILE_WIDTH), jax.random.fold_in(arg_keys[1], 1), 0, (VERTICAL_LAYERS * TILE_WIDTH) - 1).astype(jnp.int32)
    measured_tally = draw_measured_tally(jax.random.fold_in(arg_keys[5], 71), 0)
    measured_datum = centred(arg_keys[3], (MESH_HEIGHT, CBLK, OBS), 1.0, 6.0, ((0, 256),), jnp.float32)
    measured_noise_spread = jnp.clip(jnp.exp(math.log(4.0) - 2.7725887 * jax.random.uniform(arg_keys[4], (MESH_HEIGHT, CBLK, OBS), jnp.float32) ** levels(arg_keys[4], (MESH_HEIGHT, CBLK, OBS), ((0, 256),), -0.2, 0.2)), 0.25, 4.0).astype(jnp.bfloat16)
    return {"prior_sample": prior_sample, "measured_position": measured_position, "measured_tally": measured_tally, "measured_datum": measured_datum, "measured_noise_spread": measured_noise_spread}


def split_row(ocean_quantities):
    sample_total, level_count, columns = ocean_quantities.shape
    return ocean_quantities.reshape(sample_total, level_count, columns // TILE_WIDTH, TILE_WIDTH).transpose(2, 0, 1, 3).reshape(columns // TILE_WIDTH, sample_total, level_count * TILE_WIDTH)

def ocean_along_line(prior_sample, mesh_line):
    ocean_quantities = lax.dynamic_index_in_dim(prior_sample, mesh_line, 3, keepdims=False)
    sample_total = ocean_quantities.shape[0]
    tile_total = ocean_quantities.shape[2] // TILE_WIDTH
    average = lax.optimization_barrier(jnp.sum(ocean_quantities, axis=0, dtype=jnp.float32)) / sample_total
    anomaly = (ocean_quantities.astype(jnp.float32) - average).astype(jnp.bfloat16)
    tile_averages = average.reshape(VERTICAL_LAYERS, tile_total, TILE_WIDTH).transpose(1, 0, 2).reshape(tile_total, VERTICAL_LAYERS * TILE_WIDTH)
    return (split_row(anomaly), tile_averages)

def transform(system, forcing, sample_total):
    factor = jnp.linalg.cholesky(system)
    identity = jnp.broadcast_to(jnp.eye(sample_total, dtype=system.dtype), system.shape)
    inverse = jax.scipy.linalg.solve_triangular(factor, identity, lower=True)
    halfway = jnp.einsum('bkj,bj->bk', inverse, forcing, precision=lax.Precision.HIGHEST)
    mean_weight = jnp.einsum('bjk,bj->bk', inverse, halfway, precision=lax.Precision.HIGHEST)
    mixing = math.sqrt(sample_total - 1) * jnp.swapaxes(inverse, 1, 2) + mean_weight[:, :, None]
    return mixing.astype(jnp.bfloat16)

def reference(prior_sample, measured_position, measured_tally, measured_datum, measured_noise_spread):
    sample_total = prior_sample.shape[0]
    line_total = prior_sample.shape[3]
    tile_total = prior_sample.shape[2] // TILE_WIDTH
    slot_count = measured_position.shape[2]

    def prepare(mesh_line):
        tile_sequence, tile_averages = ocean_along_line(prior_sample, mesh_line)
        slots_here = lax.dynamic_index_in_dim(measured_position, mesh_line, 0, keepdims=False)
        count_here = lax.dynamic_index_in_dim(measured_tally, mesh_line, 0, keepdims=False)
        value_here = lax.dynamic_index_in_dim(measured_datum, mesh_line, 0, keepdims=False)
        var_here = lax.dynamic_index_in_dim(measured_noise_spread, mesh_line, 0, keepdims=False)
        ensemble = jnp.take_along_axis(tile_sequence, slots_here[:, None, :], axis=2)
        innovation = (value_here - jnp.take_along_axis(tile_averages, slots_here, axis=1)).astype(jnp.bfloat16)
        active = jnp.arange(slot_count)[None, :] < count_here[:, None]
        weights = jnp.where(active, 1.0 / var_here.astype(jnp.float32), 0.0).astype(jnp.bfloat16)
        weighted = (weights.astype(jnp.float32)[:, None, :] * ensemble.astype(jnp.float32)).astype(jnp.bfloat16)
        gram_block = jnp.einsum('bko,bjo->bkj', weighted.astype(jnp.float32), ensemble.astype(jnp.float32), precision=lax.Precision.HIGHEST)
        vector = jnp.einsum('bko,bo->bk', weighted.astype(jnp.float32), innovation.astype(jnp.float32), precision=lax.Precision.HIGHEST)
        return (gram_block, vector)
    gram_all, vectors = lax.map(prepare, jnp.arange(line_total))
    padded_gram = jnp.pad(gram_all, ((1, 1), (1, 1), (0, 0), (0, 0)))
    padded_vec = jnp.pad(vectors, ((1, 1), (1, 1), (0, 0)))

    def update(mesh_line):
        around_gram = lax.dynamic_slice_in_dim(padded_gram, mesh_line, 3, 0)
        around_vec = lax.dynamic_slice_in_dim(padded_vec, mesh_line, 3, 0)
        system = jnp.zeros((tile_total, sample_total, sample_total), jnp.float32)
        forcing = jnp.zeros((tile_total, sample_total), jnp.float32)
        for row_step in range(3):
            for col_step in range(3):
                falloff = 0.5 ** (abs(row_step - 1) + abs(col_step - 1))
                system = system + falloff * around_gram[row_step, col_step:col_step + tile_total]
                forcing = forcing + falloff * around_vec[row_step, col_step:col_step + tile_total]
        system = system + (sample_total - 1) * jnp.eye(sample_total, dtype=jnp.float32)
        mixing = transform(system, forcing, sample_total)
        tile_sequence, tile_averages = ocean_along_line(prior_sample, mesh_line)
        analyzed = jnp.einsum('bkv,bkq->bqv', tile_sequence.astype(jnp.float32), mixing.astype(jnp.float32), precision=lax.Precision.HIGHEST) + tile_averages[:, None, :]
        analyzed = analyzed.astype(jnp.bfloat16)
        return analyzed.reshape(tile_total, sample_total, VERTICAL_LAYERS, TILE_WIDTH).transpose(1, 2, 0, 3).reshape(sample_total, VERTICAL_LAYERS, tile_total * TILE_WIDTH)
    result = lax.map(update, jnp.arange(line_total))
    return result.transpose(1, 2, 3, 0)
```

```python
import math

import jax
import jax.numpy as jnp
from jax import lax
from jax.experimental import pallas as pl
from jax.experimental.pallas import tpu as pltpu
from jax.sharding import PartitionSpec as P

TILE_WIDTH = 128
MEM = ("mem", "tile")
VMEM_LIMIT = 48 * 1024 * 1024
F32 = jnp.float32
BF16 = jnp.bfloat16
NT = (((1,), (1,)), ((), ()))
NN = (((1,), (0,)), ((), ()))


def dot(a, b, dims=NN):
    return lax.dot_general(a, b, dims, preferred_element_type=F32)


def dot_full(a, b, dims=NN):
    return lax.dot_general(
        a, b, dims, precision=lax.Precision.HIGHEST, preferred_element_type=F32
    )


def call(body, out_shape, in_specs=None, scratch=()):
    extra = {} if in_specs is None else {"in_specs": in_specs}
    return pl.pallas_call(
        body,
        out_shape=out_shape,
        scratch_shapes=scratch,
        compiler_params=pltpu.CompilerParams(vmem_limit_bytes=VMEM_LIMIT),
        **extra,
    )


def eye(rows, cols, shift=0):
    down = lax.broadcasted_iota(jnp.int32, (rows, cols), 0)
    along = lax.broadcasted_iota(jnp.int32, (rows, cols), 1)
    return jnp.where(along == down + shift, 1.0, 0.0).astype(F32)


def split_kernel(x_ref, out_ref, wide_ref):
    rows = x_ref.shape[1]
    unit = eye(rows, rows).astype(BF16)
    for g in range(16):
        both = jnp.concatenate(
            [x_ref[g * 64 : (g + 1) * 64, :], x_ref[(16 + g) * 64 : (17 + g) * 64, :]], axis=0
        )
        wide_ref[pl.ds(g, rows, stride=16), :] = dot(unit, both, NT)
    for r in range(0, rows, 32):
        out_ref[r : r + 32] = (
            wide_ref[r * 16 : (r + 32) * 16, :].astype(BF16).reshape(32, 16, 128)
        )


def merge_kernel(x_ref, out_ref, wide_ref):
    rows = x_ref.shape[0]
    for r in range(0, rows, 32):
        wide_ref[r * 16 : (r + 32) * 16, :] = x_ref[r : r + 32].reshape(32 * 16, 128).astype(F32)
    unit = eye(128, 128).astype(BF16)
    for g in range(16):
        part = wide_ref[pl.ds(g, rows, stride=16), :].astype(BF16)
        turned = dot(unit, part, NT).astype(BF16)
        out_ref[g * 64 : (g + 1) * 64, :] = turned[:64]
        out_ref[(16 + g) * 64 : (17 + g) * 64, :] = turned[64:]


def swap_halves(low, high):
    left = lax.broadcasted_iota(jnp.int32, low.shape, low.ndim - 1) < 64
    axis = low.ndim - 1
    first = jnp.where(left, low, pltpu.roll(high, 64, axis))
    second = jnp.where(left, pltpu.roll(low, 64, axis), high)
    return first, second


def observe_kernel(x_ref, pos_ref, datum_ref, noise_ref, tally_ref, anom_ref, avg_ref, pack_ref):
    members = anom_ref.shape[1]
    groups = x_ref.shape[0]
    for c in range(2):
        for tp in range(8):
            low = x_ref[:, c * 8 + tp, 0].astype(F32)
            high = x_ref[:, c * 8 + tp, 1].astype(F32)
            first, second = swap_halves(low, high)
            cells = jnp.concatenate([first, second], axis=1).reshape(groups * 32, 128)
            average = jnp.sum(cells, axis=0, keepdims=True) / members
            anom_ref[c, :, tp * 128 : (tp + 1) * 128] = (cells - average).astype(BF16)
            avg_ref[c, :, tp * 128 : (tp + 1) * 128] = average
        pos = pos_ref[c : c + 1, :]
        level, col = pos // 128, pos % 128
        place = (col // 8) * 64 + level * 8 + col % 8
        slots = pos.shape[1]
        cell_total = anom_ref.shape[2]
        chosen = lax.broadcasted_iota(jnp.int32, (cell_total, slots), 0) == place
        chosen = jnp.where(chosen, 1.0, 0.0).astype(BF16)
        pack_ref[c, :members, :] = dot(anom_ref[c], chosen).astype(BF16)
        average = avg_ref[c]
        top = average.astype(BF16)
        rest = average - top.astype(F32)
        middle = rest.astype(BF16)
        bottom = (rest - middle.astype(F32)).astype(BF16)
        pieces = jnp.concatenate(
            [top.astype(F32), middle.astype(F32), bottom.astype(F32)]
            + [jnp.zeros((13, cell_total), F32)],
            axis=0,
        ).astype(BF16)
        found = dot(pieces, chosen)
        found = found[0:1] + (found[1:2] + found[2:3])
        innovation = datum_ref[c : c + 1, :] - found
        live = lax.broadcasted_iota(jnp.int32, (1, slots), 1) < tally_ref[0, c]
        weights = jnp.where(live, 1.0 / noise_ref[c : c + 1, :].astype(F32), 0.0)
        sub = lax.broadcasted_iota(jnp.int32, (16, slots), 0)
        tail = jnp.where(sub == 0, innovation, jnp.where(sub == 1, weights, 0.0))
        pack_ref[c, members:, :] = tail.astype(BF16)


def invert64(rows):
    n = rows[0].shape[0]
    shape = (n, 8, 128)
    sub = lax.broadcasted_iota(jnp.int32, shape, 1)

    def lane(x, j):
        return jnp.broadcast_to(x[:, :, j : j + 1], shape)

    def sublane(x, i):
        return jnp.broadcast_to(x[:, i : i + 1, :], shape)

    rows = list(rows)
    for b in range(8):
        cols = {
            (i, j): lane(rows[i], 64 + 8 * b + j) for i in range(b, 8) for j in range(8)
        }
        pivots = None
        for r in range(8):
            pivot = sublane(cols[b, r], r)
            pivots = pivot if r == 0 else jnp.where(sub == r, pivot, pivots)
            inverse = 1.0 / pivot
            heads = {j: sublane(cols[b, j], r) for j in range(r + 1, 8)}
            factors = {}
            for i in range(b, 8):
                factor = cols[i, r] * inverse
                if i == b:
                    factor = jnp.where(sub > r, factor, 0.0)
                factors[i] = factor
            for i in range(b, 8):
                for j in range(r + 1, 8):
                    cols[i, j] = cols[i, j] - factors[i] * heads[j]
            row = sublane(rows[b], r)
            for i in range(b, 8):
                if i == b and r == 7:
                    continue
                rows[i] = rows[i] - factors[i] * row
        rows[b] = rows[b] * lax.rsqrt(pivots)
    return rows


def invert128(systems):
    n = len(systems)
    left = lax.broadcasted_iota(jnp.int32, (64, 128), 1) < 64
    unit_left = eye(64, 128)
    unit_right = eye(64, 128, 64)

    def run(blocks):
        stack = [
            jnp.stack([blk[8 * i : 8 * i + 8] for blk in blocks]) for i in range(8)
        ]
        done = invert64(stack)
        return [jnp.concatenate([done[i][m] for i in range(8)], axis=0) for m in range(n)]

    upper = [s[:64] for s in systems]
    first = run([jnp.where(left, unit_left, pltpu.roll(u, 64, 1)) for u in upper])
    tops = [jnp.where(left, f, 0.0) for f in first]
    firsts = [f[:, :64] for f in first]
    across = [dot_full(f, u) for f, u in zip(firsts, upper)]
    down = [dot_full(s[64:, :64], f, NT) for s, f in zip(systems, firsts)]
    lower = [s[64:] - dot_full(d, a) for s, d, a in zip(systems, down, across)]
    second = run([jnp.where(left, unit_left, low) for low in lower])
    joined = [
        jnp.where(left, -dot_full(d, t), unit_right) for d, t in zip(down, tops)
    ]
    bottoms = [dot_full(s[:, :64], j) for s, j in zip(second, joined)]
    return [jnp.concatenate([t, b], axis=0) for t, b in zip(tops, bottoms)]


def update_kernel(own_ref, up_ref, down_ref, anom_ref, avg_ref, out_ref):
    members = anom_ref.shape[1]
    groups = members // 32
    grams, forces = [], []
    for c in range(2):
        ens, wtd, inn = [], [], []
        for ref, falloff in ((own_ref, 1.0), (up_ref, 0.5), (down_ref, 0.5)):
            ensemble = ref[c, :members, :]
            tail = ref[c, members:, :]
            weights = tail[1:2, :].astype(F32)
            weighted = (weights * ensemble.astype(F32)).astype(BF16)
            ens.append(ensemble)
            wtd.append((weighted.astype(F32) * falloff).astype(BF16))
            inn.append(tail)
        ens = jnp.concatenate(ens, axis=1)
        wtd = jnp.concatenate(wtd, axis=1)
        inn = jnp.concatenate(inn, axis=1)
        grams.append(0.5 * (dot(wtd, ens, NT) + dot(ens, wtd, NT)))
        forces.append(dot(inn, wtd, NT)[0:1])
    spread = (members - 1) * eye(members, members)
    systems = [spread + (grams[c] + 0.5 * grams[1 - c]) for c in range(2)]
    forces = [forces[c] + 0.5 * forces[1 - c] for c in range(2)]
    tops = invert128([s[:128, :128] for s in systems])
    across = [dot_full(t, s[:128, 128:]) for t, s in zip(tops, systems)]
    down = [dot_full(s[128:, :128], t, NT) for t, s in zip(tops, systems)]
    lower = [s[128:, 128:] - dot_full(d, a) for s, d, a in zip(systems, down, across)]
    lows = invert128(lower)
    mixed = [dot_full(d, t) for d, t in zip(down, tops)]
    corners = [-dot_full(low, m) for low, m in zip(lows, mixed)]
    for c in range(2):
        top = jnp.concatenate([tops[c], jnp.zeros((128, 128), F32)], axis=1)
        bottom = jnp.concatenate([corners[c], lows[c]], axis=1)
        inverse = jnp.concatenate([top, bottom], axis=0)
        halfway = jnp.sum(inverse * forces[c], axis=1, keepdims=True)
        mean_weight = jnp.sum(inverse * halfway, axis=0, keepdims=True)
        mixing = (math.sqrt(members - 1) * inverse + mean_weight).astype(BF16)
        for tp in range(8):
            span = slice(tp * 128, (tp + 1) * 128)
            made = dot(mixing, anom_ref[c, :, span]) + avg_ref[c, :, span]
            made = made.reshape(groups, 32, 128)
            low, high = swap_halves(made[:, :16], made[:, 16:])
            out_ref[:, c * 8 + tp, 0] = low.astype(BF16)
            out_ref[:, c * 8 + tp, 1] = high.astype(BF16)


def on_device(
    prior_sample, measured_position, measured_tally, measured_datum, measured_noise_spread
):
    part, level_count, width, line_total = prior_sample.shape
    groups, tiles = lax.axis_size("mem"), lax.axis_size("tile")
    members = groups * part
    cells = level_count * TILE_WIDTH
    slots = measured_position.shape[2]
    chunk = (line_total, 16, 128)
    wide = [pltpu.VMEM((line_total * 16, 128), F32)]

    parted = call(split_kernel, jax.ShapeDtypeStruct(chunk, BF16), scratch=wide)(
        prior_sample.reshape(part * level_count * width, line_total)
    )
    relaid = lax.all_to_all(parted, MEM, split_axis=0, concat_axis=0, tiled=True)

    vmem = pl.BlockSpec(memory_space=pltpu.VMEM)
    anomaly, average, packed = call(
        observe_kernel,
        (
            jax.ShapeDtypeStruct((2, members, cells), BF16),
            jax.ShapeDtypeStruct((2, 1, cells), F32),
            jax.ShapeDtypeStruct((2, members + 16, slots), BF16),
        ),
        in_specs=[vmem, vmem, vmem, vmem, pl.BlockSpec(memory_space=pltpu.SMEM)],
    )(
        relaid.reshape(groups, tiles // 2, 2, 16, 128),
        measured_position[0],
        measured_datum[0],
        measured_noise_spread[0],
        measured_tally,
    )
    ends = line_total - 1
    above = lax.ppermute(packed, MEM, [(i, i + 1) for i in range(ends)])
    below = lax.ppermute(packed, MEM, [(i + 1, i) for i in range(ends)])
    analyzed = call(
        update_kernel,
        jax.ShapeDtypeStruct((groups, tiles // 2, 2, 16, 128), BF16),
    )(packed, above, below, anomaly, average)
    returned = lax.all_to_all(
        analyzed.reshape(chunk), MEM, split_axis=0, concat_axis=0, tiled=True
    )
    merged = call(
        merge_kernel,
        jax.ShapeDtypeStruct((part * level_count * width, line_total), BF16),
        scratch=wide,
    )(returned)
    return merged.reshape(part, level_count, width, line_total)


def solution(mesh):
    placed = (
        P("mem", None, "tile", None),
        P(MEM, None, None),
        P(MEM, None),
        P(MEM, None, None),
        P(MEM, None, None),
    )
    return jax.shard_map(
        on_device,
        mesh=mesh,
        in_specs=placed,
        out_specs=P("mem", None, "tile", None),
        check_vma=False,
    )
```

```python
import math

import jax
import jax.numpy as jnp
import numpy as np
from jax import lax
from jax.experimental import pallas as pl
from jax.experimental.pallas import tpu as pltpu
from jax.sharding import PartitionSpec as P

TILE_WIDTH = 128
MEM = ("mem", "tile")
VMEM_LIMIT = 48 * 1024 * 1024
F32 = jnp.float32
BF16 = jnp.bfloat16
NT = (((1,), (1,)), ((), ()))
NN = (((1,), (0,)), ((), ()))


def dot(a, b, dims=NN):
    return lax.dot_general(a, b, dims, preferred_element_type=F32)


def dot_full(a, b, dims=NN):
    return lax.dot_general(
        a, b, dims, precision=lax.Precision.HIGHEST, preferred_element_type=F32
    )


def call(body, out_shape, in_specs=None, out_specs=None, scratch=(), cost=None):
    extra = {} if in_specs is None else {"in_specs": in_specs}
    if out_specs is not None:
        extra["out_specs"] = out_specs
    return pl.pallas_call(
        body,
        out_shape=out_shape,
        scratch_shapes=scratch,
        cost_estimate=cost,
        compiler_params=pltpu.CompilerParams(vmem_limit_bytes=VMEM_LIMIT),
        **extra,
    )


def eye(rows, cols, shift=0):
    down = lax.broadcasted_iota(jnp.int32, (rows, cols), 0)
    along = lax.broadcasted_iota(jnp.int32, (rows, cols), 1)
    return jnp.where(along == down + shift, 1.0, 0.0).astype(F32)


def row_of(device):
    x, core, z, y = device // 64, device // 32 % 2, device // 4 % 8, device % 4
    along_y = y + (x % 2) * (3 - 2 * y)
    along_z = z + (along_y % 2) * (7 - 2 * z)
    return 2 * (x * 32 + along_y * 8 + along_z) + core


def row_choice(total):
    device = lax.broadcasted_iota(jnp.int32, (total, total), 0)
    row = lax.broadcasted_iota(jnp.int32, (total, total), 1)
    return jnp.where(row == row_of(device), 1.0, 0.0).astype(BF16)


PIECES = 4


def split_kernel(
    x_ref, pos_ref, datum_ref, noise_ref, tally_ref, out_ref, obs_ref, held_ref, wide_ref, sems
):
    rows = x_ref.shape[2]
    span = x_ref.shape[1] // PIECES
    copies = [
        pltpu.make_async_copy(
            x_ref.at[:, pl.ds(i * span, span), :], held_ref.at[i], sems.at[i]
        )
        for i in range(PIECES)
    ]
    for copy in copies:
        copy.start()
    choice = row_choice(rows)
    slots = pos_ref.shape[1]
    pos = pos_ref[...]
    level, col = pos // 128, pos % 128
    obs_ref[0:2, :] = ((col // 8) * 64 + level * 8 + col % 8).astype(F32)
    obs_ref[2:4, :] = datum_ref[...]
    slot = lax.broadcasted_iota(jnp.int32, (1, slots), 1)
    for c in range(2):
        weights = 1.0 / noise_ref[c : c + 1, :].astype(F32)
        obs_ref[4 + c : 5 + c, :] = jnp.where(slot < tally_ref[0, c], weights, 0.0)
    obs_ref[6:8, :] = jnp.zeros((2, slots), F32)
    for i in range(PIECES):
        copies[i].wait()
        for h in range(span // 64):
            both = held_ref[i, :, h * 64 : (h + 1) * 64, :].reshape(128, rows)
            g = i * (span // 64) + h
            wide_ref[pl.ds(g, rows, stride=16), :] = dot(choice, both, NT)
    for r in range(0, rows, 32):
        out_ref[r : r + 32] = (
            wide_ref[r * 16 : (r + 32) * 16, :].astype(BF16).reshape(32, 16, 128)
        )


def merge_kernel(x_ref, out_ref, held_ref, wide_ref, sems):
    rows = x_ref.shape[0]
    span = out_ref.shape[1] // PIECES
    for r in range(0, rows, 32):
        wide_ref[r * 16 : (r + 32) * 16, :] = x_ref[r : r + 32].reshape(32 * 16, 128).astype(F32)
    choice = row_choice(rows)
    unit = eye(128, 128).astype(BF16)
    copies = []
    for i in range(PIECES):
        for h in range(span // 64):
            g = i * (span // 64) + h
            part = wide_ref[pl.ds(g, rows, stride=16), :].astype(BF16)
            turned = dot(dot(unit, part, NT).astype(BF16), choice).astype(BF16)
            held_ref[i, :, h * 64 : (h + 1) * 64, :] = turned.reshape(2, 64, rows)
        copy = pltpu.make_async_copy(
            held_ref.at[i], out_ref.at[:, pl.ds(i * span, span), :], sems.at[i]
        )
        copy.start()
        copies.append(copy)
    for copy in copies:
        copy.wait()


def swap_halves(low, high):
    left = lax.broadcasted_iota(jnp.int32, low.shape, low.ndim - 1) < 64
    axis = low.ndim - 1
    first = jnp.where(left, low, pltpu.roll(high, 64, axis))
    second = jnp.where(left, pltpu.roll(low, 64, axis), high)
    return first, second


def observe_kernel(x_ref, obs_ref, anom_ref, avg_ref, pack_ref):
    members = anom_ref.shape[1]
    groups = x_ref.shape[0]
    cell_total = anom_ref.shape[2]
    slots = pack_ref.shape[2]
    for c in range(2):
        for tp in range(8):
            low = x_ref[:, c * 8 + tp, 0].astype(F32)
            high = x_ref[:, c * 8 + tp, 1].astype(F32)
            first, second = swap_halves(low, high)
            cells = jnp.concatenate([first, second], axis=1).reshape(groups * 32, 128)
            average = jnp.sum(cells, axis=0, keepdims=True) / members
            anom_ref[c, :, tp * 128 : (tp + 1) * 128] = (cells - average).astype(BF16)
            avg_ref[c, :, tp * 128 : (tp + 1) * 128] = average
        place = obs_ref[c : c + 1, :].astype(jnp.int32)
        chosen = lax.broadcasted_iota(jnp.int32, (cell_total, slots), 0) == place
        chosen = jnp.where(chosen, 1.0, 0.0).astype(BF16)
        pack_ref[c, :members, :] = dot(anom_ref[c], chosen).astype(BF16)
        average = avg_ref[c]
        top = average.astype(BF16)
        rest = average - top.astype(F32)
        middle = rest.astype(BF16)
        bottom = (rest - middle.astype(F32)).astype(BF16)
        pieces = jnp.concatenate(
            [top.astype(F32), middle.astype(F32), bottom.astype(F32)]
            + [jnp.zeros((13, cell_total), F32)],
            axis=0,
        ).astype(BF16)
        found = dot(pieces, chosen)
        found = found[0:1] + (found[1:2] + found[2:3])
        innovation = obs_ref[2 + c : 3 + c, :] - found
        weights = obs_ref[4 + c : 5 + c, :]
        sub = lax.broadcasted_iota(jnp.int32, (16, slots), 0)
        tail = jnp.where(sub == 0, innovation, jnp.where(sub == 1, weights, 0.0))
        pack_ref[c, members:, :] = tail.astype(BF16)


def invert64(rows):
    n = rows[0].shape[0]
    shape = (n, 8, 128)
    sub = lax.broadcasted_iota(jnp.int32, shape, 1)

    def lane(x, j):
        return jnp.broadcast_to(x[:, :, j : j + 1], shape)

    def sublane(x, i):
        return jnp.broadcast_to(x[:, i : i + 1, :], shape)

    rows = list(rows)
    for b in range(8):
        cols = {
            (i, j): lane(rows[i], 64 + 8 * b + j) for i in range(b, 8) for j in range(8)
        }
        pivots = None
        for r in range(8):
            pivot = sublane(cols[b, r], r)
            pivots = pivot if r == 0 else jnp.where(sub == r, pivot, pivots)
            inverse = 1.0 / pivot
            heads = {j: sublane(cols[b, j], r) for j in range(r + 1, 8)}
            factors = {}
            for i in range(b, 8):
                factor = cols[i, r] * inverse
                if i == b:
                    factor = jnp.where(sub > r, factor, 0.0)
                factors[i] = factor
            for i in range(b, 8):
                for j in range(r + 1, 8):
                    cols[i, j] = cols[i, j] - factors[i] * heads[j]
            row = sublane(rows[b], r)
            for i in range(b, 8):
                if i == b and r == 7:
                    continue
                rows[i] = rows[i] - factors[i] * row
        rows[b] = rows[b] * lax.rsqrt(pivots)
    return rows


def invert128(systems):
    n = len(systems)
    left = lax.broadcasted_iota(jnp.int32, (64, 128), 1) < 64
    unit_left = eye(64, 128)
    unit_right = eye(64, 128, 64)

    def run(blocks):
        stack = [
            jnp.stack([blk[8 * i : 8 * i + 8] for blk in blocks]) for i in range(8)
        ]
        done = invert64(stack)
        return [jnp.concatenate([done[i][m] for i in range(8)], axis=0) for m in range(n)]

    upper = [s[:64] for s in systems]
    first = run([jnp.where(left, unit_left, pltpu.roll(u, 64, 1)) for u in upper])
    tops = [jnp.where(left, f, 0.0) for f in first]
    firsts = [f[:, :64] for f in first]
    across = [dot_full(f, u) for f, u in zip(firsts, upper)]
    down = [dot_full(s[64:, :64], f, NT) for s, f in zip(systems, firsts)]
    lower = [s[64:] - dot_full(d, a) for s, d, a in zip(systems, down, across)]
    second = run([jnp.where(left, unit_left, low) for low in lower])
    joined = [
        jnp.where(left, -dot_full(d, t), unit_right) for d, t in zip(down, tops)
    ]
    bottoms = [dot_full(s[:, :64], j) for s, j in zip(second, joined)]
    return [jnp.concatenate([t, b], axis=0) for t, b in zip(tops, bottoms)]


def tapered(sources, members):
    grams, forces = [], []
    for c in range(2):
        ens, wtd, inn = [], [], []
        for ref, falloff in sources:
            ensemble = ref[c, :members, :]
            tail = ref[c, members:, :]
            weights = tail[1:2, :].astype(F32)
            weighted = (weights * ensemble.astype(F32)).astype(BF16)
            ens.append(ensemble)
            wtd.append((weighted.astype(F32) * falloff).astype(BF16))
            inn.append(tail)
        if len(sources) > 1:
            ens, wtd, inn = (jnp.concatenate(p, axis=1) for p in (ens, wtd, inn))
        else:
            ens, wtd, inn = ens[0], wtd[0], inn[0]
        grams.append(0.5 * (dot(wtd, ens, NT) + dot(ens, wtd, NT)))
        forces.append(dot(inn, wtd, NT)[0:1])
    grams = [grams[c] + 0.5 * grams[1 - c] for c in range(2)]
    forces = [forces[c] + 0.5 * forces[1 - c] for c in range(2)]
    return grams, forces


def gram_kernel(own_ref, mate_ref, system_ref, force_ref):
    members = system_ref.shape[1]
    grams, forces = tapered([(own_ref, 1.0), (mate_ref, 0.5)], members)
    spread = (members - 1) * eye(members, members)
    for c in range(2):
        system_ref[c] = spread + grams[c]
        force_ref[c] = forces[c]


def update_kernel(system_ref, force_ref, far_ref, anom_ref, avg_ref, out_ref):
    members = anom_ref.shape[1]
    groups = members // 32
    grams, forces = tapered([(far_ref, 0.5)], members)
    systems = [system_ref[c] + grams[c] for c in range(2)]
    forces = [force_ref[c] + forces[c] for c in range(2)]
    tops = invert128([s[:128, :128] for s in systems])
    across = [dot_full(t, s[:128, 128:]) for t, s in zip(tops, systems)]
    down = [dot_full(s[128:, :128], t, NT) for t, s in zip(tops, systems)]
    lower = [s[128:, 128:] - dot_full(d, a) for s, d, a in zip(systems, down, across)]
    lows = invert128(lower)
    mixed = [dot_full(d, t) for d, t in zip(down, tops)]
    corners = [-dot_full(low, m) for low, m in zip(lows, mixed)]
    for c in range(2):
        top = jnp.concatenate([tops[c], jnp.zeros((128, 128), F32)], axis=1)
        bottom = jnp.concatenate([corners[c], lows[c]], axis=1)
        inverse = jnp.concatenate([top, bottom], axis=0)
        halfway = jnp.sum(inverse * forces[c], axis=1, keepdims=True)
        mean_weight = jnp.sum(inverse * halfway, axis=0, keepdims=True)
        mixing = (math.sqrt(members - 1) * inverse + mean_weight).astype(BF16)
        for tp in range(8):
            span = slice(tp * 128, (tp + 1) * 128)
            made = dot(mixing, anom_ref[c, :, span]) + avg_ref[c, :, span]
            made = made.reshape(groups, 32, 128)
            low, high = swap_halves(made[:, :16], made[:, 16:])
            out_ref[:, c * 8 + tp, 0] = low.astype(BF16)
            out_ref[:, c * 8 + tp, 1] = high.astype(BF16)


def on_device(
    prior_sample, measured_position, measured_tally, measured_datum, measured_noise_spread
):
    part, level_count, width, line_total = prior_sample.shape
    groups, tiles = lax.axis_size("mem"), lax.axis_size("tile")
    members = groups * part
    cells = level_count * TILE_WIDTH
    slots = measured_position.shape[2]
    chunk = (line_total, 16, 128)
    half = part * level_count * width // 2
    scratch = [
        pltpu.VMEM((PIECES, 2, half // PIECES, line_total), BF16),
        pltpu.VMEM((line_total * 16, 128), F32),
        pltpu.SemaphoreType.DMA((PIECES,)),
    ]
    rows = [int(r) for r in row_of(np.arange(line_total))]
    device = {r: d for d, r in enumerate(rows)}
    to_owner = [(r, device[r]) for r in range(line_total)]
    to_mate = [(device[r], device[r ^ 1]) for r in range(line_total)]
    to_far = [(device[r], device[r + 1]) for r in range(1, line_total - 1, 2)]
    to_far = to_far + [(b, a) for a, b in to_far]

    vmem = pl.BlockSpec(memory_space=pltpu.VMEM)
    anywhere = pl.BlockSpec(memory_space=pl.ANY)
    parted, observed = call(
        split_kernel,
        (jax.ShapeDtypeStruct(chunk, BF16), jax.ShapeDtypeStruct((8, slots), F32)),
        in_specs=[anywhere, vmem, vmem, vmem, pl.BlockSpec(memory_space=pltpu.SMEM)],
        scratch=scratch,
    )(
        prior_sample.reshape(2, half, line_total),
        measured_position[0],
        measured_datum[0],
        measured_noise_spread[0],
        measured_tally,
    )
    observed = lax.ppermute(observed, MEM, to_owner)
    relaid = lax.all_to_all(parted, MEM, split_axis=0, concat_axis=0, tiled=True)
    anomaly, average, packed = call(
        observe_kernel,
        (
            jax.ShapeDtypeStruct((2, members, cells), BF16),
            jax.ShapeDtypeStruct((2, 1, cells), F32),
            jax.ShapeDtypeStruct((2, members + 16, slots), BF16),
        ),
    )(relaid.reshape(groups, tiles // 2, 2, 16, 128), observed)
    far = lax.ppermute(packed, MEM, to_far)
    mate = lax.ppermute(packed, MEM, to_mate)
    system, force = call(
        gram_kernel,
        (
            jax.ShapeDtypeStruct((2, members, members), F32),
            jax.ShapeDtypeStruct((2, 1, members), F32),
        ),
        cost=pl.CostEstimate(
            flops=16 * members * members * slots, bytes_accessed=2**21, transcendentals=0
        ),
    )(packed, mate)
    analyzed = call(
        update_kernel,
        jax.ShapeDtypeStruct((groups, tiles // 2, 2, 16, 128), BF16),
    )(system, force, far, anomaly, average)
    returned = lax.all_to_all(
        analyzed.reshape(chunk), MEM, split_axis=0, concat_axis=0, tiled=True
    )
    merged = call(
        merge_kernel,
        jax.ShapeDtypeStruct((2, half, line_total), BF16),
        out_specs=anywhere,
        scratch=scratch,
    )(returned)
    return merged.reshape(part, level_count, width, line_total)


def solution(mesh):
    placed = (
        P("mem", None, "tile", None),
        P(MEM, None, None),
        P(MEM, None),
        P(MEM, None, None),
        P(MEM, None, None),
    )
    return jax.shard_map(
        on_device,
        mesh=mesh,
        in_specs=placed,
        out_specs=P("mem", None, "tile", None),
        check_vma=False,
    )
```

```python
import math

import jax
import jax.numpy as jnp
import numpy as np
from jax import lax
from jax.experimental import pallas as pl
from jax.experimental.pallas import tpu as pltpu
from jax.sharding import PartitionSpec as P

TILE_WIDTH = 128
MEM = ("mem", "tile")
VMEM_LIMIT = 48 * 1024 * 1024
F32 = jnp.float32
BF16 = jnp.bfloat16
NT = (((1,), (1,)), ((), ()))
NN = (((1,), (0,)), ((), ()))


def dot(a, b, dims=NN):
    return lax.dot_general(a, b, dims, preferred_element_type=F32)


def dot_full(a, b, dims=NN):
    return lax.dot_general(
        a, b, dims, precision=lax.Precision.HIGHEST, preferred_element_type=F32
    )


def call(body, out_shape, in_specs=None, out_specs=None, scratch=(), cost=None, limit=VMEM_LIMIT):
    extra = {} if in_specs is None else {"in_specs": in_specs}
    if out_specs is not None:
        extra["out_specs"] = out_specs
    return pl.pallas_call(
        body,
        out_shape=out_shape,
        scratch_shapes=scratch,
        cost_estimate=cost,
        compiler_params=pltpu.CompilerParams(vmem_limit_bytes=limit),
        **extra,
    )


def eye(rows, cols, shift=0):
    down = lax.broadcasted_iota(jnp.int32, (rows, cols), 0)
    along = lax.broadcasted_iota(jnp.int32, (rows, cols), 1)
    return jnp.where(along == down + shift, 1.0, 0.0).astype(F32)


def row_of(device):
    x, core, z, y = device >> 6, (device >> 5) & 1, (device >> 2) & 7, device & 3
    along_y = y + (x & 1) * (3 - 2 * y)
    along_z = z + (along_y & 1) * (7 - 2 * z)
    return 2 * (x * 32 + along_y * 8 + along_z) + core


PIECES = 8


def split_kernel(x_ref, out_ref, wide_ref):
    rows = x_ref.shape[2]
    owned = row_of(lax.broadcasted_iota(jnp.int32, (rows, 128), 0))
    along = lax.broadcasted_iota(jnp.int32, (rows, 128), 1)
    choice = jnp.concatenate(
        [jnp.where(owned == along + r, 1.0, 0.0) for r in range(0, rows, 128)], axis=1
    ).astype(BF16)
    for g in range(16):
        both = x_ref[:, g * 64 : (g + 1) * 64, :].reshape(128, rows)
        wide_ref[pl.ds(g, rows, stride=16), :] = dot(choice, both, NT)
    for d in range(0, rows, 32):
        out_ref[d : d + 32] = (
            wide_ref[d * 16 : (d + 32) * 16, :].astype(BF16).reshape(32, 16, 128)
        )


def pack_kernel(pos_ref, datum_ref, noise_ref, tally_ref, obs_ref):
    slots = pos_ref.shape[1]
    pos = pos_ref[...]
    level, col = pos >> 7, pos & 127
    obs_ref[0:2, :] = (((col >> 3) << 6) + (level << 3) + (col & 7)).astype(F32)
    obs_ref[2:4, :] = datum_ref[...]
    slot = lax.broadcasted_iota(jnp.int32, (1, slots), 1)
    for c in range(2):
        weights = 1.0 / noise_ref[c : c + 1, :].astype(F32)
        obs_ref[4 + c : 5 + c, :] = jnp.where(slot < tally_ref[0, c], weights, 0.0)
    obs_ref[6:8, :] = jnp.zeros((2, slots), F32)


def merge_kernel(x_ref, out_ref, held_ref, wide_ref, sems):
    rows = x_ref.shape[0]
    span = out_ref.shape[1] // PIECES
    for device in range(rows):
        r = row_of(device)
        wide_ref[r * 16 : (r + 1) * 16, :] = x_ref[device].astype(F32)
    unit = eye(128, 128).astype(BF16)
    copies = []
    for i in range(PIECES):
        for h in range(span // 64):
            g = i * (span // 64) + h
            part = wide_ref[pl.ds(g, rows, stride=16), :].astype(BF16)
            turned = dot(unit, part, NT).astype(BF16)
            held_ref[i, :, h * 64 : (h + 1) * 64, :] = turned.reshape(2, 64, rows)
        copy = pltpu.make_async_copy(
            held_ref.at[i], out_ref.at[:, pl.ds(i * span, span), :], sems.at[i]
        )
        copy.start()
        copies.append(copy)
    for copy in copies:
        copy.wait()


def swap_halves(low, high):
    left = lax.broadcasted_iota(jnp.int32, low.shape, low.ndim - 1) < 64
    axis = low.ndim - 1
    first = jnp.where(left, low, pltpu.roll(high, 64, axis))
    second = jnp.where(left, pltpu.roll(low, 64, axis), high)
    return first, second


def observe_kernel(x_ref, obs_ref, anom_ref, avg_ref, pack_ref):
    members = anom_ref.shape[1]
    groups = x_ref.shape[0]
    cell_total = anom_ref.shape[2]
    slots = pack_ref.shape[2]
    for c in range(2):
        for tp in range(8):
            low = x_ref[:, c * 8 + tp, 0].astype(F32)
            high = x_ref[:, c * 8 + tp, 1].astype(F32)
            first, second = swap_halves(low, high)
            cells = jnp.concatenate([first, second], axis=1).reshape(groups * 32, 128)
            average = jnp.sum(cells, axis=0, keepdims=True) / members
            anom_ref[c, :, tp * 128 : (tp + 1) * 128] = (cells - average).astype(BF16)
            avg_ref[c, :, tp * 128 : (tp + 1) * 128] = average
        place = obs_ref[c : c + 1, :].astype(jnp.int32)
        chosen = lax.broadcasted_iota(jnp.int32, (cell_total, slots), 0) == place
        chosen = jnp.where(chosen, 1.0, 0.0).astype(BF16)
        pack_ref[c, :members, :] = dot(anom_ref[c], chosen).astype(BF16)
        average = avg_ref[c]
        top = average.astype(BF16)
        rest = average - top.astype(F32)
        middle = rest.astype(BF16)
        bottom = (rest - middle.astype(F32)).astype(BF16)
        pieces = jnp.concatenate(
            [top.astype(F32), middle.astype(F32), bottom.astype(F32)]
            + [jnp.zeros((13, cell_total), F32)],
            axis=0,
        ).astype(BF16)
        found = dot(pieces, chosen)
        found = found[0:1] + (found[1:2] + found[2:3])
        innovation = obs_ref[2 + c : 3 + c, :] - found
        weights = obs_ref[4 + c : 5 + c, :]
        sub = lax.broadcasted_iota(jnp.int32, (16, slots), 0)
        tail = jnp.where(sub == 0, innovation, jnp.where(sub == 1, weights, 0.0))
        pack_ref[c, members:, :] = tail.astype(BF16)


def invert64(rows):
    shape = rows[0].shape
    sub = lax.broadcasted_iota(jnp.int32, shape, 0)
    lane = lax.broadcasted_iota(jnp.int32, shape, 1)
    half, own = lane & 64, lane & 63
    unit = jnp.where((lane & 7) == sub, 1.0, 0.0)

    def spread(x, col):
        return jnp.take_along_axis(x, half + col, axis=1)

    def sublane(x, i):
        return jnp.broadcast_to(x[i : i + 1, :], shape)

    rows = list(rows)
    following = [spread(rows[0], j) for j in range(8)]
    for b in range(8):
        cols = {(b, j): following[j] for j in range(8)}
        following = []
        for i in range(b + 1, 8):
            for j in range(8):
                cols[i, j] = spread(rows[i], 8 * b + j)
            if i == b + 1:
                following = [spread(rows[i], 8 * i + j) for j in range(8)]
        here = (own >> 3) == b
        for i in range(b, 8):
            rows[i] = jnp.where(here, unit if i == b else 0.0, rows[i])
        pivots = None
        for r in range(8):
            pivot = sublane(cols[b, r], r)
            pivots = pivot if r == 0 else jnp.where(sub == r, pivot, pivots)
            inverse = 1.0 / pivot
            factors = {}
            for i in range(b, 8):
                factor = cols[i, r] * inverse
                factors[i] = jnp.where(sub > r, factor, 0.0) if i == b else factor
            following = [
                f - factors[b + 1] * sublane(cols[b + 1, r], j) for j, f in enumerate(following)
            ]
            for j in range(r + 1, 8):
                head = sublane(cols[b, j], r)
                for i in range(b, 8):
                    cols[i, j] = cols[i, j] - factors[i] * head
            row = sublane(rows[b], r)
            for i in range(b, 8):
                if i > b or r < 7:
                    rows[i] = rows[i] - factors[i] * row
        rows[b] = jnp.where(own <= sub + 8 * b, rows[b] * lax.rsqrt(pivots), 0.0)
    return rows


def invert256(systems):
    left = lax.broadcasted_iota(jnp.int32, (64, 128), 1) < 64
    unit_right = eye(64, 128, 64)

    def turn(x):
        return pltpu.roll(x, 64, 1)

    def run(pair, right):
        low, high = pair
        both = jnp.where(left, turn(low) if right else low, high if right else turn(high))
        done = jnp.concatenate(invert64([both[8 * i : 8 * i + 8] for i in range(8)]), axis=0)
        return [jnp.where(left, done, 0.0), jnp.where(left, turn(done), 0.0)]

    first = run([s[:64, :128] for s in systems], False)
    t0 = [t[:, :64] for t in first]
    u0 = [dot_full(t, s[:64]) for t, s in zip(t0, systems)]
    m0 = [dot_full(s[64:, :64], t, NT) for t, s in zip(t0, systems)]
    s1 = [s[64:] - dot_full(m, u) for s, m, u in zip(systems, m0, u0)]

    second = run([s[:64, :128] for s in s1], True)
    t1 = [t[:, :64] for t in second]
    u1 = [dot_full(t, s[:64, 128:]) for t, s in zip(t1, s1)]
    m1 = [dot_full(s[64:, :128], turn(t), NT) for t, s in zip(second, s1)]
    s2 = [s[64:, 128:] - dot_full(m, u) for s, m, u in zip(s1, m1, u1)]
    l0 = first
    l1 = [
        dot_full(t, jnp.where(left, -dot_full(m[:64], p), unit_right))
        for t, m, p in zip(t1, m0, l0)
    ]

    third = run([s[:64] for s in s2], False)
    t2 = [t[:, :64] for t in third]
    u2 = [dot_full(t, s[:64]) for t, s in zip(t2, s2)]
    m2 = [dot_full(s[64:, :64], t, NT) for t, s in zip(t2, s2)]
    s3 = [s[64:] - dot_full(m, u) for s, m, u in zip(s2, m2, u2)]
    l2 = [
        -dot_full(t, dot_full(m[64:128], p) + dot_full(n[:64], q))
        for t, m, p, n, q in zip(t2, m0, l0, m1, l1)
    ]
    r3 = [
        dot_full(m[128:], p) + dot_full(n[64:], q) + dot_full(o, z)
        for m, p, n, q, o, z in zip(m0, l0, m1, l1, m2, l2)
    ]
    r3_right = [
        jnp.where(left, -dot_full(o, z), unit_right) for o, z in zip(m2, third)
    ]

    fourth = run(s3, True)
    t3 = [t[:, :64] for t in fourth]
    rows = []
    for c in range(2):
        last = jnp.concatenate(
            [-dot_full(t3[c], r3[c]), dot_full(t3[c], r3_right[c])], axis=1
        )
        rows.append([l0[c], l1[c], jnp.concatenate([l2[c], third[c]], axis=1), last])
    return rows


def tapered(sources, members):
    grams, forces = [], []
    for c in range(2):
        ens, wtd, inn = [], [], []
        for ref, falloff in sources:
            ensemble = ref[c, :members, :]
            tail = ref[c, members:, :]
            weights = tail[1:2, :].astype(F32)
            weighted = (weights * ensemble.astype(F32)).astype(BF16)
            ens.append(ensemble)
            wtd.append((weighted.astype(F32) * falloff).astype(BF16))
            inn.append(tail)
        if len(sources) > 1:
            ens, wtd, inn = (jnp.concatenate(p, axis=1) for p in (ens, wtd, inn))
        else:
            ens, wtd, inn = ens[0], wtd[0], inn[0]
        grams.append(0.5 * (dot(wtd, ens, NT) + dot(ens, wtd, NT)))
        forces.append(dot(inn, wtd, NT)[0:1])
    grams = [grams[c] + 0.5 * grams[1 - c] for c in range(2)]
    forces = [forces[c] + 0.5 * forces[1 - c] for c in range(2)]
    return grams, forces


def gram_kernel(own_ref, mate_ref, system_ref, force_ref):
    members = system_ref.shape[1]
    grams, forces = tapered([(own_ref, 1.0), (mate_ref, 0.5)], members)
    spread = (members - 1) * eye(members, members)
    for c in range(2):
        system_ref[c] = spread + grams[c]
        force_ref[c] = forces[c]


def update_kernel(system_ref, force_ref, far_ref, anom_ref, avg_ref, out_ref):
    members = anom_ref.shape[1]
    groups = members // 32
    grams, forces = tapered([(far_ref, 0.5)], members)
    systems = [system_ref[c] + grams[c] for c in range(2)]
    forces = [force_ref[c] + forces[c] for c in range(2)]
    inverses = invert256(systems)
    for c in range(2):
        force = forces[c]
        mean_weight = jnp.zeros((1, members), F32)
        for rows in inverses[c]:
            if rows.shape[1] < members:
                halfway = jnp.sum(rows * force[:, :128], axis=1, keepdims=True)
                part = jnp.sum(rows * halfway, axis=0, keepdims=True)
                part = jnp.concatenate([part, jnp.zeros((1, 128), F32)], axis=1)
            else:
                halfway = jnp.sum(rows * force, axis=1, keepdims=True)
                part = jnp.sum(rows * halfway, axis=0, keepdims=True)
            mean_weight = mean_weight + part
        scale = math.sqrt(members - 1)
        mixing = []
        for rows in inverses[c]:
            if rows.shape[1] < members:
                rows = jnp.concatenate([rows, jnp.zeros((64, 128), F32)], axis=1)
            mixing.append((scale * rows + mean_weight).astype(BF16))
        mixing = jnp.concatenate(mixing, axis=0)
        for tp in range(8):
            span = slice(tp * 128, (tp + 1) * 128)
            made = dot(mixing, anom_ref[c, :, span]) + avg_ref[c, :, span]
            made = made.reshape(groups, 32, 128)
            low, high = swap_halves(made[:, :16], made[:, 16:])
            out_ref[:, c * 8 + tp, 0] = low.astype(BF16)
            out_ref[:, c * 8 + tp, 1] = high.astype(BF16)


def on_device(
    prior_sample, measured_position, measured_tally, measured_datum, measured_noise_spread
):
    part, level_count, width, line_total = prior_sample.shape
    groups, tiles = lax.axis_size("mem"), lax.axis_size("tile")
    members = groups * part
    cells = level_count * TILE_WIDTH
    slots = measured_position.shape[2]
    chunk = (line_total, 16, 128)
    half = part * level_count * width // 2
    scratch = [
        pltpu.VMEM((PIECES, 2, half // PIECES, line_total), BF16),
        pltpu.VMEM((line_total * 16, 128), F32),
        pltpu.SemaphoreType.DMA((PIECES,)),
    ]
    rows = [int(r) for r in row_of(np.arange(line_total))]
    device = {r: d for d, r in enumerate(rows)}
    to_owner = [(r, device[r]) for r in range(line_total)]
    to_mate = [(device[r], device[r ^ 1]) for r in range(line_total)]
    to_far = [(device[r], device[r + 1]) for r in range(1, line_total - 1, 2)]
    to_far = to_far + [(b, a) for a, b in to_far]

    vmem = pl.BlockSpec(memory_space=pltpu.VMEM)
    anywhere = pl.BlockSpec(memory_space=pltpu.HBM)
    parted = call(
        split_kernel,
        jax.ShapeDtypeStruct(chunk, BF16),
        scratch=scratch[1:2],
    )(prior_sample.reshape(2, half, line_total))
    observed = call(
        pack_kernel,
        jax.ShapeDtypeStruct((8, slots), F32),
        in_specs=[vmem, vmem, vmem, pl.BlockSpec(memory_space=pltpu.SMEM)],
    )(measured_position[0], measured_datum[0], measured_noise_spread[0], measured_tally)
    observed = lax.ppermute(observed, MEM, to_owner)
    relaid = lax.all_to_all(parted, MEM, split_axis=0, concat_axis=0, tiled=True)
    anomaly, average, packed = call(
        observe_kernel,
        (
            jax.ShapeDtypeStruct((2, members, cells), BF16),
            jax.ShapeDtypeStruct((2, 1, cells), F32),
            jax.ShapeDtypeStruct((2, members + 16, slots), BF16),
        ),
    )(relaid.reshape(groups, tiles // 2, 2, 16, 128), observed)
    far = lax.ppermute(packed, MEM, to_far)
    mate = lax.ppermute(packed, MEM, to_mate)
    system, force = call(
        gram_kernel,
        (
            jax.ShapeDtypeStruct((2, members, members), F32),
            jax.ShapeDtypeStruct((2, 1, members), F32),
        ),
        cost=pl.CostEstimate(
            flops=16 * members * members * slots, bytes_accessed=2**21, transcendentals=0
        ),
    )(packed, mate)
    analyzed = call(
        update_kernel,
        jax.ShapeDtypeStruct((groups, tiles // 2, 2, 16, 128), BF16),
    )(system, force, far, anomaly, average)
    returned = lax.all_to_all(
        analyzed.reshape(chunk), MEM, split_axis=0, concat_axis=0, tiled=True
    )
    merged = call(
        merge_kernel,
        jax.ShapeDtypeStruct((2, half, line_total), BF16),
        out_specs=anywhere,
        scratch=scratch,
    )(returned)
    return merged.reshape(part, level_count, width, line_total)


def solution(mesh):
    placed = (
        P("mem", None, "tile", None),
        P(MEM, None, None),
        P(MEM, None),
        P(MEM, None, None),
        P(MEM, None, None),
    )
    return jax.shard_map(
        on_device,
        mesh=mesh,
        in_specs=placed,
        out_specs=P("mem", None, "tile", None),
        check_vma=False,
    )
```

```python
import math

import jax
import jax.numpy as jnp
import numpy as np
from jax import lax
from jax.experimental import pallas as pl
from jax.experimental.pallas import tpu as pltpu
from jax.sharding import PartitionSpec as P

TILE_WIDTH = 128
MEM = ("mem", "tile")
TILE_FIRST = ("tile", "mem")
VMEM_LIMIT = 48 * 1024 * 1024
F32 = jnp.float32
BF16 = jnp.bfloat16
NT = (((1,), (1,)), ((), ()))
NN = (((1,), (0,)), ((), ()))


def dot(a, b, dims=NN):
    return lax.dot_general(a, b, dims, preferred_element_type=F32)


def dot_full(a, b, dims=NN):
    return lax.dot_general(
        a, b, dims, precision=lax.Precision.HIGHEST, preferred_element_type=F32
    )


def call(body, out_shape, in_specs=None, out_specs=None, scratch=(), cost=None, limit=VMEM_LIMIT):
    extra = {} if in_specs is None else {"in_specs": in_specs}
    if out_specs is not None:
        extra["out_specs"] = out_specs
    return pl.pallas_call(
        body,
        out_shape=out_shape,
        scratch_shapes=scratch,
        cost_estimate=cost,
        compiler_params=pltpu.CompilerParams(vmem_limit_bytes=limit),
        **extra,
    )


def eye(rows, cols, shift=0):
    down = lax.broadcasted_iota(jnp.int32, (rows, cols), 0)
    along = lax.broadcasted_iota(jnp.int32, (rows, cols), 1)
    return jnp.where(along == down + shift, 1.0, 0.0).astype(F32)


def row_of(tile, mem):
    x, core, z, y = mem >> 1, mem & 1, tile >> 2, tile & 3
    along_y = y + (x & 1) * (3 - 2 * y)
    along_z = z + (along_y & 1) * (7 - 2 * z)
    return 2 * (x * 32 + along_y * 8 + along_z) + core


def row_of_chunk(chunk):
    return row_of(chunk >> 3, chunk & 7)


PIECES = 8


def split_kernel(x_ref, out_ref, held_ref, wide_ref, sems):
    rows = x_ref.shape[2]
    span = rows // PIECES
    owned = row_of_chunk(lax.broadcasted_iota(jnp.int32, (rows, 128), 0))
    along = lax.broadcasted_iota(jnp.int32, (rows, 128), 1)
    choice = jnp.concatenate(
        [jnp.where(owned == along + r, 1.0, 0.0) for r in range(0, rows, 128)], axis=1
    ).astype(BF16)
    for g in range(0, 16, 2):
        both = [
            x_ref[:, h * 64 : (h + 1) * 64, :].reshape(128, rows) for h in (g, g + 1)
        ]
        both = dot(choice, jnp.concatenate(both, axis=0), NT)
        wide_ref[pl.ds(g, rows, stride=16), :] = both[:, :128]
        wide_ref[pl.ds(g + 1, rows, stride=16), :] = both[:, 128:]
    copies = []
    for i in range(PIECES):
        d = i * span
        held_ref[i] = wide_ref[d * 16 : (d + span) * 16, :].astype(BF16).reshape(span, 16, 128)
        copy = pltpu.make_async_copy(held_ref.at[i], out_ref.at[pl.ds(d, span)], sems.at[i])
        copy.start()
        copies.append(copy)
    for copy in copies:
        copy.wait()


def pack_kernel(pos_ref, datum_ref, noise_ref, tally_ref, obs_ref):
    slots = pos_ref.shape[1]
    pos = pos_ref[...]
    level, col = pos >> 7, pos & 127
    obs_ref[0:2, :] = (((col >> 3) << 6) + (level << 3) + (col & 7)).astype(F32)
    obs_ref[2:4, :] = datum_ref[...]
    slot = lax.broadcasted_iota(jnp.int32, (1, slots), 1)
    for c in range(2):
        weights = 1.0 / noise_ref[c : c + 1, :].astype(F32)
        obs_ref[4 + c : 5 + c, :] = jnp.where(slot < tally_ref[0, c], weights, 0.0)
    obs_ref[6:8, :] = jnp.zeros((2, slots), F32)


def merge_kernel(x_ref, out_ref, held_ref, wide_ref, sems):
    rows = x_ref.shape[0]
    span = out_ref.shape[1] // PIECES
    for chunk in range(rows):
        r = row_of_chunk(chunk)
        wide_ref[r * 16 : (r + 1) * 16, :] = x_ref[chunk].astype(F32)
    unit = eye(128, 128).astype(BF16)
    copies = []
    for i in range(PIECES):
        for h in range(span // 64):
            g = i * (span // 64) + h
            part = wide_ref[pl.ds(g, rows, stride=16), :].astype(BF16)
            turned = dot(unit, part, NT).astype(BF16)
            held_ref[i, :, h * 64 : (h + 1) * 64, :] = turned.reshape(2, 64, rows)
        copy = pltpu.make_async_copy(
            held_ref.at[i], out_ref.at[:, pl.ds(i * span, span), :], sems.at[i]
        )
        copy.start()
        copies.append(copy)
    for copy in copies:
        copy.wait()


def swap_halves(low, high):
    left = lax.broadcasted_iota(jnp.int32, low.shape, low.ndim - 1) < 64
    axis = low.ndim - 1
    inner = pltpu.roll(jnp.where(left, high, low), 64, axis)
    return jnp.where(left, low, inner), jnp.where(left, inner, high)


def observe_kernel(x_ref, obs_ref, anom_ref, avg_ref, pack_ref):
    members = anom_ref.shape[1]
    groups = x_ref.shape[2]
    cell_total = anom_ref.shape[2]
    slots = pack_ref.shape[2]
    for c in range(2):
        for tp in range(8):
            low = x_ref[c * 8 + tp, 0].astype(F32)
            high = x_ref[c * 8 + tp, 1].astype(F32)
            first, second = swap_halves(low, high)
            cells = jnp.concatenate([first, second], axis=1).reshape(groups * 32, 128)
            average = jnp.sum(cells, axis=0, keepdims=True) / members
            anom_ref[c, :, tp * 128 : (tp + 1) * 128] = (cells - average).astype(BF16)
            avg_ref[c, :, tp * 128 : (tp + 1) * 128] = average
        place = obs_ref[c : c + 1, :].astype(jnp.int32)
        chosen = lax.broadcasted_iota(jnp.int32, (cell_total, slots), 0) == place
        chosen = jnp.where(chosen, 1.0, 0.0).astype(BF16)
        pack_ref[c, :members, :] = dot(anom_ref[c], chosen).astype(BF16)
        average = avg_ref[c]
        top = average.astype(BF16)
        rest = average - top.astype(F32)
        middle = rest.astype(BF16)
        bottom = (rest - middle.astype(F32)).astype(BF16)
        pieces = jnp.concatenate(
            [top.astype(F32), middle.astype(F32), bottom.astype(F32)]
            + [jnp.zeros((13, cell_total), F32)],
            axis=0,
        ).astype(BF16)
        found = dot(pieces, chosen)
        found = found[0:1] + (found[1:2] + found[2:3])
        innovation = obs_ref[2 + c : 3 + c, :] - found
        weights = obs_ref[4 + c : 5 + c, :]
        sub = lax.broadcasted_iota(jnp.int32, (16, slots), 0)
        tail = jnp.where(sub == 0, innovation, jnp.where(sub == 1, weights, 0.0))
        pack_ref[c, members:, :] = tail.astype(BF16)


def invert64(rows):
    shape = rows[0].shape
    sub = lax.broadcasted_iota(jnp.int32, shape, 0)
    lane = lax.broadcasted_iota(jnp.int32, shape, 1)
    half, own = lane & 64, lane & 63
    unit = jnp.where((lane & 7) == sub, 1.0, 0.0)

    def spread(x, col):
        return jnp.take_along_axis(x, half + col, axis=1)

    def sublane(x, i):
        return jnp.broadcast_to(x[i : i + 1, :], shape)

    rows = list(rows)
    following = [spread(rows[0], j) for j in range(8)]
    for b in range(8):
        cols = {(b, j): following[j] for j in range(8)}
        following = []
        for i in range(b + 1, 8):
            for j in range(8):
                cols[i, j] = spread(rows[i], 8 * b + j)
            if i == b + 1:
                following = [spread(rows[i], 8 * i + j) for j in range(8)]
        here = (own >> 3) == b
        for i in range(b, 8):
            rows[i] = jnp.where(here, unit if i == b else 0.0, rows[i])
        pivots = None
        for r in range(8):
            pivot = sublane(cols[b, r], r)
            pivots = pivot if r == 0 else jnp.where(sub == r, pivot, pivots)
            inverse = 1.0 / pivot
            factors = {}
            for i in range(b, 8):
                factor = cols[i, r] * inverse
                factors[i] = jnp.where(sub > r, factor, 0.0) if i == b else factor
            following = [
                f - factors[b + 1] * sublane(cols[b + 1, r], j) for j, f in enumerate(following)
            ]
            for j in range(r + 1, 8):
                head = sublane(cols[b, j], r)
                for i in range(b, 8):
                    cols[i, j] = cols[i, j] - factors[i] * head
            row = sublane(rows[b], r)
            for i in range(b, 8):
                if i > b or r < 7:
                    rows[i] = rows[i] - factors[i] * row
        rows[b] = jnp.where(own <= sub + 8 * b, rows[b] * lax.rsqrt(pivots), 0.0)
    return rows


def invert256(systems):
    left = lax.broadcasted_iota(jnp.int32, (64, 128), 1) < 64
    unit_right = eye(64, 128, 64)

    def turn(x):
        return pltpu.roll(x, 64, 1)

    def run(pair, right):
        low, high = pair
        both = jnp.where(left, turn(low) if right else low, high if right else turn(high))
        done = jnp.concatenate(invert64([both[8 * i : 8 * i + 8] for i in range(8)]), axis=0)
        return [jnp.where(left, done, 0.0), jnp.where(left, turn(done), 0.0)]

    first = run([s[:64, :128] for s in systems], False)
    t0 = [t[:, :64] for t in first]
    u0 = [dot_full(t, s[:64, :128]) for t, s in zip(t0, systems)]
    m0 = [dot_full(s[64:128, :64], t, NT) for t, s in zip(t0, systems)]
    s1 = [s[64:128, :128] - dot_full(m, u) for s, m, u in zip(systems, m0, u0)]

    second = run(s1, True)
    v0 = [dot_full(t, s[:64, 128:]) for t, s in zip(t0, systems)]
    n0 = [dot_full(s[128:, :64], t, NT) for t, s in zip(t0, systems)]
    up1 = [s[64:128, 128:] - dot_full(m, v) for s, m, v in zip(systems, m0, v0)]
    down1 = [s[128:, :128] - dot_full(n, u) for s, n, u in zip(systems, n0, u0)]
    rest = [s[128:, 128:] - dot_full(n, v) for s, n, v in zip(systems, n0, v0)]
    t1 = [t[:, :64] for t in second]
    u1 = [dot_full(t, u) for t, u in zip(t1, up1)]
    m1 = [dot_full(d, turn(t), NT) for t, d in zip(second, down1)]
    s2 = [s[:64] - dot_full(m[:64], u) for s, m, u in zip(rest, m1, u1)]

    third = run(s2, False)
    low2 = [s[64:] - dot_full(m[64:], u) for s, m, u in zip(rest, m1, u1)]
    l0 = first
    l1 = [
        dot_full(t, jnp.where(left, -dot_full(m, p), unit_right))
        for t, m, p in zip(t1, m0, l0)
    ]
    r2 = [
        dot_full(n, p) + dot_full(m, q) for n, p, m, q in zip(n0, l0, m1, l1)
    ]
    t2 = [t[:, :64] for t in third]
    u2 = [dot_full(t, s) for t, s in zip(t2, s2)]
    m2 = [dot_full(s[:, :64], t, NT) for t, s in zip(t2, low2)]
    s3 = [s - dot_full(m, u) for s, m, u in zip(low2, m2, u2)]

    fourth = run(s3, True)
    l2 = [-dot_full(t, r[:64]) for t, r in zip(t2, r2)]
    r3 = [r[64:] + dot_full(m, p) for r, m, p in zip(r2, m2, l2)]
    r3_right = [jnp.where(left, -dot_full(m, p), unit_right) for m, p in zip(m2, third)]
    t3 = [t[:, :64] for t in fourth]
    rows = []
    for c in range(2):
        last = jnp.concatenate(
            [-dot_full(t3[c], r3[c]), dot_full(t3[c], r3_right[c])], axis=1
        )
        rows.append([l0[c], l1[c], jnp.concatenate([l2[c], third[c]], axis=1), last])
    return rows


def tapered(refs, falloff, members):
    grams, forces = [], []
    for c in range(2):
        ens, wtd, inn = [], [], []
        for ref in refs:
            ensemble = ref[c, :members, :]
            tail = ref[c, members:, :]
            weights = tail[1:2, :].astype(F32)
            ens.append(ensemble)
            wtd.append((weights * ensemble.astype(F32)).astype(BF16))
            inn.append(tail)
        if len(refs) > 1:
            ens, wtd, inn = (jnp.concatenate(p, axis=1) for p in (ens, wtd, inn))
        else:
            ens, wtd, inn = ens[0], wtd[0], inn[0]
        grams.append(0.5 * falloff * (dot(wtd, ens, NT) + dot(ens, wtd, NT)))
        forces.append(falloff * dot(inn, wtd, NT)[0:1])
    grams = [grams[c] + 0.5 * grams[1 - c] for c in range(2)]
    forces = [forces[c] + 0.5 * forces[1 - c] for c in range(2)]
    return grams, forces


def gram_kernel(own_ref, system_ref, force_ref, hand_ref):
    members = system_ref.shape[1]
    hand_ref[...] = own_ref[...]
    grams, forces = tapered([own_ref], 1.0, members)
    spread = (members - 1) * eye(members, members)
    for c in range(2):
        system_ref[c] = spread + grams[c]
        force_ref[c] = forces[c]


def update_kernel(system_ref, force_ref, mate_ref, far_ref, anom_ref, avg_ref, out_ref):
    members = anom_ref.shape[1]
    groups = members // 32
    grams, forces = tapered([mate_ref, far_ref], 0.5, members)
    systems = [system_ref[c] + grams[c] for c in range(2)]
    forces = [force_ref[c] + forces[c] for c in range(2)]
    inverses = invert256(systems)
    for c in range(2):
        force = forces[c]
        mean_weight = jnp.zeros((1, members), F32)
        for rows in inverses[c]:
            if rows.shape[1] < members:
                halfway = jnp.sum(rows * force[:, :128], axis=1, keepdims=True)
                part = jnp.sum(rows * halfway, axis=0, keepdims=True)
                part = jnp.concatenate([part, jnp.zeros((1, 128), F32)], axis=1)
            else:
                halfway = jnp.sum(rows * force, axis=1, keepdims=True)
                part = jnp.sum(rows * halfway, axis=0, keepdims=True)
            mean_weight = mean_weight + part
        scale = math.sqrt(members - 1)
        mixing = []
        for rows in inverses[c]:
            if rows.shape[1] < members:
                rows = jnp.concatenate([rows, jnp.zeros((64, 128), F32)], axis=1)
            mixing.append((scale * rows + mean_weight).astype(BF16))
        mixing = jnp.concatenate(mixing, axis=0)
        for tp in range(0, 8, 2):
            span = slice(tp * 128, (tp + 2) * 128)
            made = dot(mixing, anom_ref[c, :, span]) + avg_ref[c, :, span]
            for h in range(2):
                part = made[:, h * 128 : (h + 1) * 128].reshape(groups, 32, 128)
                low, high = swap_halves(part[:, :16], part[:, 16:])
                out_ref[c * 8 + tp + h, 0] = low.astype(BF16)
                out_ref[c * 8 + tp + h, 1] = high.astype(BF16)


def on_device(
    prior_sample, measured_position, measured_tally, measured_datum, measured_noise_spread
):
    part, level_count, width, line_total = prior_sample.shape
    groups, tiles = lax.axis_size("mem"), lax.axis_size("tile")
    members = groups * part
    cells = level_count * TILE_WIDTH
    slots = measured_position.shape[2]
    chunk = (line_total, 16, 128)
    paired = (tiles // 2, 2, groups, 16, 128)
    half = part * level_count * width // 2
    scratch = [
        pltpu.VMEM((PIECES, 2, half // PIECES, line_total), BF16),
        pltpu.VMEM((line_total * 16, 128), F32),
        pltpu.SemaphoreType.DMA((PIECES,)),
    ]
    places = np.arange(line_total)
    rows = [int(r) for r in row_of(places % tiles, places // tiles)]
    device = {r: d for d, r in enumerate(rows)}
    to_owner = [(r, device[r]) for r in range(line_total)]
    to_mate = [(device[r], device[r ^ 1]) for r in range(line_total)]
    to_far = [(device[r], device[r + 1]) for r in range(1, line_total - 1, 2)]
    to_far = to_far + [(b, a) for a, b in to_far]

    vmem = pl.BlockSpec(memory_space=pltpu.VMEM)
    anywhere = pl.BlockSpec(memory_space=pltpu.HBM)
    parted = call(
        split_kernel,
        jax.ShapeDtypeStruct(chunk, BF16),
        out_specs=anywhere,
        scratch=[pltpu.VMEM((PIECES, line_total // PIECES, 16, 128), BF16)] + scratch[1:],
    )(prior_sample.reshape(2, half, line_total))
    observed = call(
        pack_kernel,
        jax.ShapeDtypeStruct((8, slots), F32),
        in_specs=[vmem, vmem, vmem, pl.BlockSpec(memory_space=pltpu.SMEM)],
    )(measured_position[0], measured_datum[0], measured_noise_spread[0], measured_tally)
    observed = lax.ppermute(observed, MEM, to_owner)
    relaid = lax.all_to_all(parted, TILE_FIRST, split_axis=0, concat_axis=0, tiled=True)
    anomaly, average, packed = call(
        observe_kernel,
        (
            jax.ShapeDtypeStruct((2, members, cells), BF16),
            jax.ShapeDtypeStruct((2, 1, cells), F32),
            jax.ShapeDtypeStruct((2, members + 16, slots), BF16),
        ),
    )(relaid.reshape(paired), observed)
    far = lax.ppermute(packed, MEM, to_far)
    system, force, hand = call(
        gram_kernel,
        (
            jax.ShapeDtypeStruct((2, members, members), F32),
            jax.ShapeDtypeStruct((2, 1, members), F32),
            jax.ShapeDtypeStruct(packed.shape, BF16),
        ),
    )(packed)
    mate = lax.ppermute(hand, MEM, to_mate)
    analyzed = call(
        update_kernel,
        jax.ShapeDtypeStruct(paired, BF16),
    )(system, force, mate, far, anomaly, average)
    returned = lax.all_to_all(
        analyzed.reshape(chunk), TILE_FIRST, split_axis=0, concat_axis=0, tiled=True
    )
    merged = call(
        merge_kernel,
        jax.ShapeDtypeStruct((2, half, line_total), BF16),
        out_specs=anywhere,
        scratch=scratch,
    )(returned)
    return merged.reshape(part, level_count, width, line_total)


def solution(mesh):
    placed = (
        P("mem", None, "tile", None),
        P(MEM, None, None),
        P(MEM, None),
        P(MEM, None, None),
        P(MEM, None, None),
    )
    return jax.shard_map(
        on_device,
        mesh=mesh,
        in_specs=placed,
        out_specs=P("mem", None, "tile", None),
        check_vma=False,
    )
```

```python
import math

import jax
import jax.numpy as jnp
import numpy as np
from jax import lax
from jax.experimental import pallas as pl
from jax.experimental.pallas import tpu as pltpu
from jax.sharding import PartitionSpec as P

TILE_WIDTH = 128
MEM = ("mem", "tile")
TILE_FIRST = ("tile", "mem")
VMEM_LIMIT = 48 * 1024 * 1024
F32 = jnp.float32
BF16 = jnp.bfloat16
NT = (((1,), (1,)), ((), ()))
NN = (((1,), (0,)), ((), ()))


def dot(a, b, dims=NN):
    return lax.dot_general(a, b, dims, preferred_element_type=F32)


def dot_full(a, b, dims=NN):
    return lax.dot_general(
        a, b, dims, precision=lax.Precision.HIGHEST, preferred_element_type=F32
    )


def call(body, out_shape, in_specs=None, out_specs=None, scratch=(), cost=None, limit=VMEM_LIMIT):
    extra = {} if in_specs is None else {"in_specs": in_specs}
    if out_specs is not None:
        extra["out_specs"] = out_specs
    return pl.pallas_call(
        body,
        out_shape=out_shape,
        scratch_shapes=scratch,
        cost_estimate=cost,
        compiler_params=pltpu.CompilerParams(vmem_limit_bytes=limit),
        **extra,
    )


def eye(rows, cols, shift=0):
    down = lax.broadcasted_iota(jnp.int32, (rows, cols), 0)
    along = lax.broadcasted_iota(jnp.int32, (rows, cols), 1)
    return jnp.where(along == down + shift, 1.0, 0.0).astype(F32)


def row_of(tile, mem):
    x, core, z, y = mem >> 1, mem & 1, tile >> 2, tile & 3
    along_y = y + (x & 1) * (3 - 2 * y)
    along_z = z + (along_y & 1) * (7 - 2 * z)
    return 2 * (x * 32 + along_y * 8 + along_z) + core


def row_of_chunk(chunk):
    return row_of(chunk >> 3, chunk & 7)


PIECES = 8


def split_kernel(x_ref, out_ref, held_ref, wide_ref, sems):
    rows = x_ref.shape[2]
    span = rows // PIECES
    owned = row_of_chunk(lax.broadcasted_iota(jnp.int32, (rows, 128), 0))
    along = lax.broadcasted_iota(jnp.int32, (rows, 128), 1)
    choice = jnp.concatenate(
        [jnp.where(owned == along + r, 1.0, 0.0) for r in range(0, rows, 128)], axis=1
    ).astype(BF16)
    for g in range(0, 16, 2):
        both = [
            x_ref[:, h * 64 : (h + 1) * 64, :].reshape(128, rows) for h in (g, g + 1)
        ]
        both = dot(choice, jnp.concatenate(both, axis=0), NT)
        wide_ref[pl.ds(g, rows, stride=16), :] = both[:, :128]
        wide_ref[pl.ds(g + 1, rows, stride=16), :] = both[:, 128:]
    copies = []
    for i in range(PIECES):
        d = i * span
        held_ref[i] = wide_ref[d * 16 : (d + span) * 16, :].astype(BF16).reshape(span, 16, 128)
        copy = pltpu.make_async_copy(held_ref.at[i], out_ref.at[pl.ds(d, span)], sems.at[i])
        copy.start()
        copies.append(copy)
    for copy in copies:
        copy.wait()


def pack_kernel(pos_ref, datum_ref, noise_ref, tally_ref, obs_ref):
    slots = pos_ref.shape[1]
    pos = pos_ref[...]
    level, col = pos >> 7, pos & 127
    obs_ref[0:2, :] = (((col >> 3) << 6) + (level << 3) + (col & 7)).astype(F32)
    obs_ref[2:4, :] = datum_ref[...]
    slot = lax.broadcasted_iota(jnp.int32, (1, slots), 1)
    for c in range(2):
        weights = 1.0 / noise_ref[c : c + 1, :].astype(F32)
        obs_ref[4 + c : 5 + c, :] = jnp.where(slot < tally_ref[0, c], weights, 0.0)
    obs_ref[6:8, :] = jnp.zeros((2, slots), F32)


def merge_kernel(x_ref, out_ref, held_ref, wide_ref, sems):
    rows = x_ref.shape[0]
    span = out_ref.shape[1] // PIECES
    for chunk in range(rows):
        r = row_of_chunk(chunk)
        wide_ref[r * 16 : (r + 1) * 16, :] = x_ref[chunk].astype(F32)
    unit = eye(128, 128).astype(BF16)
    copies = []
    for i in range(PIECES):
        for h in range(span // 64):
            g = i * (span // 64) + h
            part = wide_ref[pl.ds(g, rows, stride=16), :].astype(BF16)
            turned = dot(unit, part, NT).astype(BF16)
            held_ref[i, :, h * 64 : (h + 1) * 64, :] = turned.reshape(2, 64, rows)
        copy = pltpu.make_async_copy(
            held_ref.at[i], out_ref.at[:, pl.ds(i * span, span), :], sems.at[i]
        )
        copy.start()
        copies.append(copy)
    for copy in copies:
        copy.wait()


def swap_halves(low, high):
    left = lax.broadcasted_iota(jnp.int32, low.shape, low.ndim - 1) < 64
    axis = low.ndim - 1
    inner = pltpu.roll(jnp.where(left, high, low), 64, axis)
    return jnp.where(left, low, inner), jnp.where(left, inner, high)


def observe_kernel(x_ref, obs_ref, anom_ref, avg_ref, pack_ref):
    members = anom_ref.shape[1]
    groups = x_ref.shape[2]
    cell_total = anom_ref.shape[2]
    slots = pack_ref.shape[2]
    for c in range(2):
        for tp in range(8):
            low = x_ref[c * 8 + tp, 0].astype(F32)
            high = x_ref[c * 8 + tp, 1].astype(F32)
            first, second = swap_halves(low, high)
            cells = jnp.concatenate([first, second], axis=1).reshape(groups * 32, 128)
            average = jnp.sum(cells, axis=0, keepdims=True) / members
            anom_ref[c, :, tp * 128 : (tp + 1) * 128] = (cells - average).astype(BF16)
            avg_ref[c, :, tp * 128 : (tp + 1) * 128] = average
        place = obs_ref[c : c + 1, :].astype(jnp.int32)
        chosen = lax.broadcasted_iota(jnp.int32, (cell_total, slots), 0) == place
        chosen = jnp.where(chosen, 1.0, 0.0).astype(BF16)
        pack_ref[c, :members, :] = dot(anom_ref[c], chosen).astype(BF16)
        average = avg_ref[c]
        top = average.astype(BF16)
        rest = average - top.astype(F32)
        middle = rest.astype(BF16)
        bottom = (rest - middle.astype(F32)).astype(BF16)
        pieces = jnp.concatenate(
            [top.astype(F32), middle.astype(F32), bottom.astype(F32)]
            + [jnp.zeros((13, cell_total), F32)],
            axis=0,
        ).astype(BF16)
        found = dot(pieces, chosen)
        found = found[0:1] + (found[1:2] + found[2:3])
        innovation = obs_ref[2 + c : 3 + c, :] - found
        weights = obs_ref[4 + c : 5 + c, :]
        sub = lax.broadcasted_iota(jnp.int32, (16, slots), 0)
        tail = jnp.where(sub == 0, innovation, jnp.where(sub == 1, weights, 0.0))
        pack_ref[c, members:, :] = tail.astype(BF16)


def invert64(rows):
    shape = rows[0].shape
    sub = lax.broadcasted_iota(jnp.int32, shape, 0)
    lane = lax.broadcasted_iota(jnp.int32, shape, 1)
    half, own = lane & 64, lane & 63
    unit = jnp.where((lane & 7) == sub, 1.0, 0.0)

    def spread(x, col):
        return jnp.take_along_axis(x, half + col, axis=1)

    def sublane(x, i):
        return jnp.broadcast_to(x[i : i + 1, :], shape)

    rows = list(rows)
    following = [spread(rows[0], j) for j in range(8)]
    for b in range(8):
        cols = {(b, j): following[j] for j in range(8)}
        following = []
        for i in range(b + 1, 8):
            for j in range(8):
                cols[i, j] = spread(rows[i], 8 * b + j)
            if i == b + 1:
                following = [spread(rows[i], 8 * i + j) for j in range(8)]
        here = (own >> 3) == b
        for i in range(b, 8):
            rows[i] = jnp.where(here, unit if i == b else 0.0, rows[i])
        pivots = None
        for r in range(8):
            pivot = sublane(cols[b, r], r)
            pivots = pivot if r == 0 else jnp.where(sub == r, pivot, pivots)
            inverse = 1.0 / pivot
            factors = {}
            for i in range(b, 8):
                factor = cols[i, r] * inverse
                factors[i] = jnp.where(sub > r, factor, 0.0) if i == b else factor
            following = [
                f - factors[b + 1] * sublane(cols[b + 1, r], j) for j, f in enumerate(following)
            ]
            for j in range(r + 1, 8):
                head = sublane(cols[b, j], r)
                cols[b, j] = cols[b, j] - (cols[b, r] * head) * inverse
                for i in range(b + 1, 8):
                    cols[i, j] = cols[i, j] - factors[i] * head
            row = sublane(rows[b], r)
            for i in range(b, 8):
                if i > b or r < 7:
                    rows[i] = rows[i] - factors[i] * row
        rows[b] = jnp.where(own <= sub + 8 * b, rows[b] * lax.rsqrt(pivots), 0.0)
    return rows


def invert256(systems, low, high):
    left = lax.broadcasted_iota(jnp.int32, (64, 128), 1) < 64
    unit_right = eye(64, 128, 64)

    def turn(x):
        return pltpu.roll(x, 64, 1)

    def run(low, high):
        both = jnp.where(left, low, high)
        done = jnp.concatenate(invert64([both[8 * i : 8 * i + 8] for i in range(8)]), axis=0)
        return jnp.where(left, done, 0.0), jnp.where(left, 0.0, done)

    def times(t, half, x):
        if half:
            return dot_full(t, jnp.concatenate([jnp.zeros(x.shape, F32), x], axis=0))
        return dot_full(t[:, :64], x)

    def times_t(x, t, half):
        return dot_full(x, t, NT) if half else dot_full(x[:, :64], t[:, :64], NT)

    two = range(2)
    near = [s[:, :128] for s in systems]
    turned = [turn(x) for x in near]
    swapped = [turned[0], near[1]]
    facing = [near[0], turned[1]]

    t0 = run(low, high)
    u0 = [times(t0[c], c, swapped[c][:64]) for c in two]
    m0 = [times_t(facing[c][64:128], t0[c], c) for c in two]
    s1 = [swapped[c][64:128] - dot_full(m0[c], u0[c]) for c in two]

    t1 = run(*s1)
    v0 = [times(t0[c], c, systems[c][:64, 128:]) for c in two]
    n0 = [times_t(facing[c][128:], t0[c], c) for c in two]
    up1 = [systems[c][64:128, 128:] - dot_full(m0[c], v0[c]) for c in two]
    down1 = [swapped[c][128:] - dot_full(n0[c], u0[c]) for c in two]
    rest = [systems[c][128:, 128:] - dot_full(n0[c], v0[c]) for c in two]
    up1, rest = [up1[0], turn(up1[1])], [rest[0], turn(rest[1])]
    u1 = [times(t1[c], c, up1[c]) for c in two]
    m1 = [times_t(down1[c], t1[c], c) for c in two]
    s2 = [rest[c][:64] - dot_full(m1[c][:64], u1[c]) for c in two]

    t2 = run(*s2)
    low2 = [rest[c][64:] - dot_full(m1[c][64:], u1[c]) for c in two]
    l0 = [t0[0], turn(t0[1])]
    l1 = [
        times(t1[c], c, jnp.where(left, -dot_full(m0[c], l0[c]), unit_right)) for c in two
    ]
    r2 = [dot_full(n0[c], l0[c]) + dot_full(m1[c], l1[c]) for c in two]
    u2 = [times(t2[c], c, s2[c]) for c in two]
    m2 = [times_t(low2[c], t2[c], c) for c in two]
    s3 = [low2[c] - dot_full(m2[c], u2[c]) for c in two]

    t3 = run(s3[1], s3[0])[::-1]
    third = [t2[0], turn(t2[1])]
    l2 = [-times(t2[c], c, r2[c][:64]) for c in two]
    r3 = [r2[c][64:] + dot_full(m2[c], l2[c]) for c in two]
    r3_right = [jnp.where(left, -dot_full(m2[c], third[c]), unit_right) for c in two]
    rows = []
    for c in two:
        last = times(t3[c], 1 - c, jnp.concatenate([-r3[c], r3_right[c]], axis=1))
        rows.append([l0[c], l1[c], jnp.concatenate([l2[c], third[c]], axis=1), last])
    return rows


def observed_block(refs, c, members):
    ens, wtd, inn = [], [], []
    for ref in refs:
        ensemble = ref[c, :members, :]
        tail = ref[c, members:, :]
        weights = tail[1:2, :].astype(F32)
        ens.append(ensemble)
        wtd.append((weights * ensemble.astype(F32)).astype(BF16))
        inn.append(tail)
    if len(refs) > 1:
        return tuple(jnp.concatenate(p, axis=1) for p in (ens, wtd, inn))
    return ens[0], wtd[0], inn[0]


def tapered(blocks, falloff, rows, spans):
    def pick(x):
        return jnp.concatenate([x[at] for at in spans], axis=0) if len(spans) > 1 else x[spans[0]]

    grams = [
        0.5 * falloff * (dot(wtd[rows], pick(ens), NT) + dot(ens[rows], pick(wtd), NT))
        for ens, wtd, _ in blocks
    ]
    return [grams[c] + 0.5 * grams[1 - c] for c in range(2)]


def tapered_forcing(blocks, falloff):
    forces = [falloff * dot(inn, wtd, NT)[0:1] for _, wtd, inn in blocks]
    return [forces[c] + 0.5 * forces[1 - c] for c in range(2)]


def gram_kernel(own_ref, system_ref, force_ref, hand_ref):
    members = system_ref.shape[1]
    hand_ref[...] = own_ref[...]
    blocks = [observed_block([own_ref], c, members) for c in range(2)]
    grams = tapered(blocks, 1.0, slice(0, members), [slice(0, members)])
    forces = tapered_forcing(blocks, 1.0)
    spread = (members - 1) * eye(members, members)
    for c in range(2):
        system_ref[c] = spread + grams[c]
        force_ref[c] = forces[c]


def update_kernel(system_ref, force_ref, mate_ref, far_ref, anom_ref, avg_ref, out_ref):
    members = anom_ref.shape[1]
    groups = members // 32
    blocks = [observed_block([mate_ref, far_ref], c, members) for c in range(2)]
    head, whole = slice(0, 64), slice(0, members)
    low = tapered(blocks, 0.5, head, [slice(0, 128)])[0]
    high = tapered(blocks, 0.5, head, [slice(64, 128), slice(0, 64)])[1]
    low = system_ref[0, :64, :128] + low
    high = pltpu.roll(system_ref[1, :64, :128], 64, 1) + high
    grams = tapered(blocks, 0.5, whole, [whole])
    systems = [system_ref[c] + grams[c] for c in range(2)]
    forces = tapered_forcing(blocks, 0.5)
    forces = [force_ref[c] + forces[c] for c in range(2)]
    inverses = invert256(systems, low, high)
    for c in range(2):
        force = forces[c]
        mean_weight = jnp.zeros((1, members), F32)
        for rows in inverses[c]:
            if rows.shape[1] < members:
                halfway = jnp.sum(rows * force[:, :128], axis=1, keepdims=True)
                part = jnp.sum(rows * halfway, axis=0, keepdims=True)
                part = jnp.concatenate([part, jnp.zeros((1, 128), F32)], axis=1)
            else:
                halfway = jnp.sum(rows * force, axis=1, keepdims=True)
                part = jnp.sum(rows * halfway, axis=0, keepdims=True)
            mean_weight = mean_weight + part
        scale = math.sqrt(members - 1)
        mixing = []
        for rows in inverses[c]:
            if rows.shape[1] < members:
                rows = jnp.concatenate([rows, jnp.zeros((64, 128), F32)], axis=1)
            mixing.append((scale * rows + mean_weight).astype(BF16))
        mixing = jnp.concatenate(mixing, axis=0)
        for tp in range(0, 8, 2):
            span = slice(tp * 128, (tp + 2) * 128)
            made = dot(mixing, anom_ref[c, :, span]) + avg_ref[c, :, span]
            for h in range(2):
                part = made[:, h * 128 : (h + 1) * 128].reshape(groups, 32, 128)
                low, high = swap_halves(part[:, :16], part[:, 16:])
                out_ref[c * 8 + tp + h, 0] = low.astype(BF16)
                out_ref[c * 8 + tp + h, 1] = high.astype(BF16)


def on_device(
    prior_sample, measured_position, measured_tally, measured_datum, measured_noise_spread
):
    part, level_count, width, line_total = prior_sample.shape
    groups, tiles = lax.axis_size("mem"), lax.axis_size("tile")
    members = groups * part
    cells = level_count * TILE_WIDTH
    slots = measured_position.shape[2]
    chunk = (line_total, 16, 128)
    paired = (tiles // 2, 2, groups, 16, 128)
    half = part * level_count * width // 2
    scratch = [
        pltpu.VMEM((PIECES, 2, half // PIECES, line_total), BF16),
        pltpu.VMEM((line_total * 16, 128), F32),
        pltpu.SemaphoreType.DMA((PIECES,)),
    ]
    places = np.arange(line_total)
    rows = [int(r) for r in row_of(places % tiles, places // tiles)]
    device = {r: d for d, r in enumerate(rows)}
    to_owner = [(r, device[r]) for r in range(line_total)]
    to_mate = [(device[r], device[r ^ 1]) for r in range(line_total)]
    to_far = [(device[r], device[r + 1]) for r in range(1, line_total - 1, 2)]
    to_far = to_far + [(b, a) for a, b in to_far]

    vmem = pl.BlockSpec(memory_space=pltpu.VMEM)
    anywhere = pl.BlockSpec(memory_space=pltpu.HBM)
    parted = call(
        split_kernel,
        jax.ShapeDtypeStruct(chunk, BF16),
        out_specs=anywhere,
        scratch=[pltpu.VMEM((PIECES, line_total // PIECES, 16, 128), BF16)] + scratch[1:],
    )(prior_sample.reshape(2, half, line_total))
    observed = call(
        pack_kernel,
        jax.ShapeDtypeStruct((8, slots), F32),
        in_specs=[vmem, vmem, vmem, pl.BlockSpec(memory_space=pltpu.SMEM)],
    )(measured_position[0], measured_datum[0], measured_noise_spread[0], measured_tally)
    observed = lax.ppermute(observed, MEM, to_owner)
    relaid = lax.all_to_all(parted, TILE_FIRST, split_axis=0, concat_axis=0, tiled=True)
    anomaly, average, packed = call(
        observe_kernel,
        (
            jax.ShapeDtypeStruct((2, members, cells), BF16),
            jax.ShapeDtypeStruct((2, 1, cells), F32),
            jax.ShapeDtypeStruct((2, members + 16, slots), BF16),
        ),
    )(relaid.reshape(paired), observed)
    far = lax.ppermute(packed, MEM, to_far)
    system, force, hand = call(
        gram_kernel,
        (
            jax.ShapeDtypeStruct((2, members, members), F32),
            jax.ShapeDtypeStruct((2, 1, members), F32),
            jax.ShapeDtypeStruct(packed.shape, BF16),
        ),
    )(packed)
    mate = lax.ppermute(hand, MEM, to_mate)
    analyzed = call(
        update_kernel,
        jax.ShapeDtypeStruct(paired, BF16),
    )(system, force, mate, far, anomaly, average)
    returned = lax.all_to_all(
        analyzed.reshape(chunk), TILE_FIRST, split_axis=0, concat_axis=0, tiled=True
    )
    merged = call(
        merge_kernel,
        jax.ShapeDtypeStruct((2, half, line_total), BF16),
        out_specs=anywhere,
        scratch=scratch,
    )(returned)
    return merged.reshape(part, level_count, width, line_total)


def solution(mesh):
    placed = (
        P("mem", None, "tile", None),
        P(MEM, None, None),
        P(MEM, None),
        P(MEM, None, None),
        P(MEM, None, None),
    )
    return jax.shard_map(
        on_device,
        mesh=mesh,
        in_specs=placed,
        out_specs=P("mem", None, "tile", None),
        check_vma=False,
    )
```

```python
import math

import jax
import jax.numpy as jnp
import numpy as np
from jax import lax
from jax.experimental import pallas as pl
from jax.experimental.pallas import tpu as pltpu
from jax.sharding import PartitionSpec as P

TILE_WIDTH = 128
MEM = ("mem", "tile")
TILE_FIRST = ("tile", "mem")
VMEM_LIMIT = 48 * 1024 * 1024
F32 = jnp.float32
BF16 = jnp.bfloat16
NT = (((1,), (1,)), ((), ()))
NN = (((1,), (0,)), ((), ()))


def dot(a, b, dims=NN):
    return lax.dot_general(a, b, dims, preferred_element_type=F32)


def dot_full(a, b, dims=NN):
    return lax.dot_general(
        a, b, dims, precision=lax.Precision.HIGHEST, preferred_element_type=F32
    )


def call(body, out_shape, in_specs=None, out_specs=None, scratch=(), cost=None, limit=VMEM_LIMIT):
    extra = {} if in_specs is None else {"in_specs": in_specs}
    if out_specs is not None:
        extra["out_specs"] = out_specs
    return pl.pallas_call(
        body,
        out_shape=out_shape,
        scratch_shapes=scratch,
        cost_estimate=cost,
        compiler_params=pltpu.CompilerParams(vmem_limit_bytes=limit),
        **extra,
    )


def eye(rows, cols, shift=0):
    down = lax.broadcasted_iota(jnp.int32, (rows, cols), 0)
    along = lax.broadcasted_iota(jnp.int32, (rows, cols), 1)
    return jnp.where(along == down + shift, 1.0, 0.0).astype(F32)


def row_of(tile, mem):
    x, core, z, y = mem >> 1, mem & 1, tile >> 2, tile & 3
    along_y = y + (x & 1) * (3 - 2 * y)
    along_z = z + (along_y & 1) * (7 - 2 * z)
    return 2 * (x * 32 + along_y * 8 + along_z) + core


def row_of_chunk(chunk):
    return row_of(chunk >> 3, chunk & 7)


PIECES = 8


def split_kernel(x_ref, out_ref, held_ref, wide_ref, sems):
    rows = x_ref.shape[2]
    span = rows // PIECES
    owned = row_of_chunk(lax.broadcasted_iota(jnp.int32, (rows, 128), 0))
    along = lax.broadcasted_iota(jnp.int32, (rows, 128), 1)
    choice = jnp.concatenate(
        [jnp.where(owned == along + r, 1.0, 0.0) for r in range(0, rows, 128)], axis=1
    ).astype(BF16)
    for g in range(0, 16, 2):
        both = [
            x_ref[:, h * 64 : (h + 1) * 64, :].reshape(128, rows) for h in (g, g + 1)
        ]
        both = dot(choice, jnp.concatenate(both, axis=0), NT)
        wide_ref[pl.ds(g, rows, stride=16), :] = both[:, :128]
        wide_ref[pl.ds(g + 1, rows, stride=16), :] = both[:, 128:]
    copies = []
    for i in range(PIECES):
        d = i * span
        held_ref[i] = wide_ref[d * 16 : (d + span) * 16, :].astype(BF16).reshape(span, 16, 128)
        copy = pltpu.make_async_copy(held_ref.at[i], out_ref.at[pl.ds(d, span)], sems.at[i])
        copy.start()
        copies.append(copy)
    for copy in copies:
        copy.wait()


def pack_kernel(pos_ref, datum_ref, noise_ref, tally_ref, obs_ref):
    slots = pos_ref.shape[1]
    pos = pos_ref[...]
    level, col = pos >> 7, pos & 127
    obs_ref[0:2, :] = (((col >> 3) << 6) + (level << 3) + (col & 7)).astype(F32)
    obs_ref[2:4, :] = datum_ref[...]
    slot = lax.broadcasted_iota(jnp.int32, (1, slots), 1)
    for c in range(2):
        weights = 1.0 / noise_ref[c : c + 1, :].astype(F32)
        obs_ref[4 + c : 5 + c, :] = jnp.where(slot < tally_ref[0, c], weights, 0.0)
    obs_ref[6:8, :] = jnp.zeros((2, slots), F32)


def merge_kernel(x_ref, out_ref, held_ref, wide_ref, sems):
    rows = x_ref.shape[0]
    span = out_ref.shape[1] // PIECES
    for chunk in range(rows):
        r = row_of_chunk(chunk)
        wide_ref[r * 16 : (r + 1) * 16, :] = x_ref[chunk].astype(F32)
    unit = eye(128, 128).astype(BF16)
    copies = []
    for i in range(PIECES):
        for h in range(span // 64):
            g = i * (span // 64) + h
            part = wide_ref[pl.ds(g, rows, stride=16), :].astype(BF16)
            turned = dot(unit, part, NT).astype(BF16)
            held_ref[i, :, h * 64 : (h + 1) * 64, :] = turned.reshape(2, 64, rows)
        copy = pltpu.make_async_copy(
            held_ref.at[i], out_ref.at[:, pl.ds(i * span, span), :], sems.at[i]
        )
        copy.start()
        copies.append(copy)
    for copy in copies:
        copy.wait()


def swap_halves(low, high):
    left = lax.broadcasted_iota(jnp.int32, low.shape, low.ndim - 1) < 64
    axis = low.ndim - 1
    inner = pltpu.roll(jnp.where(left, high, low), 64, axis)
    return jnp.where(left, low, inner), jnp.where(left, inner, high)


def observe_kernel(x_ref, obs_ref, cells_ref, pack_ref):
    members = cells_ref.shape[1]
    cell_total = cells_ref.shape[2]
    slots = pack_ref.shape[2]
    for c in range(2):
        for tp in range(8):
            first, second = swap_halves(x_ref[c * 8 + tp, 0], x_ref[c * 8 + tp, 1])
            cells = jnp.concatenate([first, second], axis=1).reshape(members, 128)
            cells_ref[c, :, tp * 128 : (tp + 1) * 128] = cells
        place = obs_ref[c : c + 1, :].astype(jnp.int32)
        chosen = lax.broadcasted_iota(jnp.int32, (cell_total, slots), 0) == place
        chosen = jnp.where(chosen, 1.0, 0.0).astype(BF16)
        found = dot(cells_ref[c], chosen)
        average = jnp.sum(found, axis=0, keepdims=True) / members
        pack_ref[c, :members, :] = (found - average).astype(BF16)
        innovation = obs_ref[2 + c : 3 + c, :] - average
        weights = obs_ref[4 + c : 5 + c, :]
        sub = lax.broadcasted_iota(jnp.int32, (16, slots), 0)
        tail = jnp.where(sub == 0, innovation, jnp.where(sub == 1, weights, 0.0))
        pack_ref[c, members:, :] = tail.astype(BF16)


def invert64(rows):
    shape = rows[0].shape
    sub = lax.broadcasted_iota(jnp.int32, shape, 0)
    lane = lax.broadcasted_iota(jnp.int32, shape, 1)
    half, own = lane & 64, lane & 63
    unit = jnp.where((lane & 7) == sub, 1.0, 0.0)

    def spread(x, col):
        return jnp.take_along_axis(x, half + col, axis=1)

    def sublane(x, i):
        return jnp.broadcast_to(x[i : i + 1, :], shape)

    rows = list(rows)
    following = [spread(rows[0], j) for j in range(8)]
    for b in range(8):
        cols = {(b, j): following[j] for j in range(8)}
        following = []
        for i in range(b + 1, 8):
            for j in range(8):
                cols[i, j] = spread(rows[i], 8 * b + j)
            if i == b + 1:
                following = [spread(rows[i], 8 * i + j) for j in range(8)]
        here = (own >> 3) == b
        for i in range(b, 8):
            rows[i] = jnp.where(here, unit if i == b else 0.0, rows[i])
        pivots = None
        for r in range(8):
            pivot = sublane(cols[b, r], r)
            pivots = pivot if r == 0 else jnp.where(sub == r, pivot, pivots)
            inverse = 1.0 / pivot
            factors = {}
            for i in range(b, 8):
                factor = cols[i, r] * inverse
                factors[i] = jnp.where(sub > r, factor, 0.0) if i == b else factor
            following = [
                f - factors[b + 1] * sublane(cols[b + 1, r], j) for j, f in enumerate(following)
            ]
            for j in range(r + 1, 8):
                head = sublane(cols[b, j], r)
                cols[b, j] = cols[b, j] - (cols[b, r] * head) * inverse
                for i in range(b + 1, 8):
                    cols[i, j] = cols[i, j] - factors[i] * head
            row = sublane(rows[b], r)
            for i in range(b, 8):
                if i > b or r < 7:
                    rows[i] = rows[i] - factors[i] * row
        rows[b] = jnp.where(own <= sub + 8 * b, rows[b] * lax.rsqrt(pivots), 0.0)
    return rows


def invert256(systems, low, high):
    left = lax.broadcasted_iota(jnp.int32, (64, 128), 1) < 64
    unit_right = eye(64, 128, 64)

    def turn(x):
        return pltpu.roll(x, 64, 1)

    def run(low, high):
        both = jnp.where(left, low, high)
        done = jnp.concatenate(invert64([both[8 * i : 8 * i + 8] for i in range(8)]), axis=0)
        return jnp.where(left, done, 0.0), jnp.where(left, 0.0, done)

    def times(t, half, x):
        if half:
            return dot_full(t, jnp.concatenate([jnp.zeros(x.shape, F32), x], axis=0))
        return dot_full(t[:, :64], x)

    def times_t(x, t, half):
        return dot_full(x, t, NT) if half else dot_full(x[:, :64], t[:, :64], NT)

    two = range(2)
    near = [s[:, :128] for s in systems]
    turned = [turn(x) for x in near]
    swapped = [turned[0], near[1]]
    facing = [near[0], turned[1]]

    t0 = run(low, high)
    u0 = [times(t0[c], c, swapped[c][:64]) for c in two]
    m0 = [times_t(facing[c][64:128], t0[c], c) for c in two]
    s1 = [swapped[c][64:128] - dot_full(m0[c], u0[c]) for c in two]

    t1 = run(*s1)
    v0 = [times(t0[c], c, systems[c][:64, 128:]) for c in two]
    n0 = [times_t(facing[c][128:], t0[c], c) for c in two]
    up1 = [systems[c][64:128, 128:] - dot_full(m0[c], v0[c]) for c in two]
    down1 = [swapped[c][128:] - dot_full(n0[c], u0[c]) for c in two]
    rest = [systems[c][128:, 128:] - dot_full(n0[c], v0[c]) for c in two]
    up1, rest = [up1[0], turn(up1[1])], [rest[0], turn(rest[1])]
    u1 = [times(t1[c], c, up1[c]) for c in two]
    m1 = [times_t(down1[c], t1[c], c) for c in two]
    s2 = [rest[c][:64] - dot_full(m1[c][:64], u1[c]) for c in two]

    t2 = run(*s2)
    low2 = [rest[c][64:] - dot_full(m1[c][64:], u1[c]) for c in two]
    l0 = [t0[0], turn(t0[1])]
    l1 = [
        times(t1[c], c, jnp.where(left, -dot_full(m0[c], l0[c]), unit_right)) for c in two
    ]
    r2 = [dot_full(n0[c], l0[c]) + dot_full(m1[c], l1[c]) for c in two]
    u2 = [times(t2[c], c, s2[c]) for c in two]
    m2 = [times_t(low2[c], t2[c], c) for c in two]
    s3 = [low2[c] - dot_full(m2[c], u2[c]) for c in two]

    t3 = run(s3[1], s3[0])[::-1]
    third = [t2[0], turn(t2[1])]
    l2 = [-times(t2[c], c, r2[c][:64]) for c in two]
    r3 = [r2[c][64:] + dot_full(m2[c], l2[c]) for c in two]
    r3_right = [jnp.where(left, -dot_full(m2[c], third[c]), unit_right) for c in two]
    rows = []
    for c in two:
        last = times(t3[c], 1 - c, jnp.concatenate([-r3[c], r3_right[c]], axis=1))
        rows.append([l0[c], l1[c], jnp.concatenate([l2[c], third[c]], axis=1), last])
    return rows


def observed_block(refs, c, members):
    ens, wtd, inn = [], [], []
    for ref in refs:
        ensemble = ref[c, :members, :]
        tail = ref[c, members:, :]
        weights = tail[1:2, :].astype(F32)
        ens.append(ensemble)
        wtd.append((weights * ensemble.astype(F32)).astype(BF16))
        inn.append(tail)
    if len(refs) > 1:
        return tuple(jnp.concatenate(p, axis=1) for p in (ens, wtd, inn))
    return ens[0], wtd[0], inn[0]


def tapered(blocks, falloff, rows, spans):
    def pick(x):
        return jnp.concatenate([x[at] for at in spans], axis=0) if len(spans) > 1 else x[spans[0]]

    grams = [
        0.5 * falloff * (dot(wtd[rows], pick(ens), NT) + dot(ens[rows], pick(wtd), NT))
        for ens, wtd, _ in blocks
    ]
    return [grams[c] + 0.5 * grams[1 - c] for c in range(2)]


def tapered_forcing(blocks, falloff):
    forces = [falloff * dot(inn, wtd, NT)[0:1] for _, wtd, inn in blocks]
    return [forces[c] + 0.5 * forces[1 - c] for c in range(2)]


def gram_kernel(own_ref, system_ref, force_ref, hand_ref):
    members = system_ref.shape[1]
    hand_ref[...] = own_ref[...]
    blocks = [observed_block([own_ref], c, members) for c in range(2)]
    grams = tapered(blocks, 1.0, slice(0, members), [slice(0, members)])
    forces = tapered_forcing(blocks, 1.0)
    spread = (members - 1) * eye(members, members)
    for c in range(2):
        system_ref[c] = spread + grams[c]
        force_ref[c] = forces[c]


def anomaly_kernel(cells_ref, force_ref, anom_ref, avg_ref, same_ref):
    members = cells_ref.shape[1]
    same_ref[...] = force_ref[...]
    for c in range(2):
        for at in range(0, cells_ref.shape[2], 128):
            cells = cells_ref[c, :, at : at + 128].astype(F32)
            average = jnp.sum(cells, axis=0, keepdims=True) / members
            anom_ref[c, :, at : at + 128] = (cells - average).astype(BF16)
            avg_ref[c, :, at : at + 128] = average


def update_kernel(system_ref, force_ref, mate_ref, far_ref, anom_ref, avg_ref, out_ref):
    members = anom_ref.shape[1]
    groups = members // 32
    blocks = [observed_block([mate_ref, far_ref], c, members) for c in range(2)]
    head, whole = slice(0, 64), slice(0, members)
    low = tapered(blocks, 0.5, head, [slice(0, 128)])[0]
    high = tapered(blocks, 0.5, head, [slice(64, 128), slice(0, 64)])[1]
    low = system_ref[0, :64, :128] + low
    high = pltpu.roll(system_ref[1, :64, :128], 64, 1) + high
    grams = tapered(blocks, 0.5, whole, [whole])
    systems = [system_ref[c] + grams[c] for c in range(2)]
    forces = tapered_forcing(blocks, 0.5)
    forces = [force_ref[c] + forces[c] for c in range(2)]
    inverses = invert256(systems, low, high)
    for c in range(2):
        force = forces[c]
        mean_weight = jnp.zeros((1, members), F32)
        for rows in inverses[c]:
            if rows.shape[1] < members:
                halfway = jnp.sum(rows * force[:, :128], axis=1, keepdims=True)
                part = jnp.sum(rows * halfway, axis=0, keepdims=True)
                part = jnp.concatenate([part, jnp.zeros((1, 128), F32)], axis=1)
            else:
                halfway = jnp.sum(rows * force, axis=1, keepdims=True)
                part = jnp.sum(rows * halfway, axis=0, keepdims=True)
            mean_weight = mean_weight + part
        scale = math.sqrt(members - 1)
        mixing = []
        for rows in inverses[c]:
            if rows.shape[1] < members:
                rows = jnp.concatenate([rows, jnp.zeros((64, 128), F32)], axis=1)
            mixing.append((scale * rows + mean_weight).astype(BF16))
        mixing = jnp.concatenate(mixing, axis=0)
        for tp in range(0, 8, 2):
            span = slice(tp * 128, (tp + 2) * 128)
            made = dot(mixing, anom_ref[c, :, span]) + avg_ref[c, :, span]
            for h in range(2):
                part = made[:, h * 128 : (h + 1) * 128].reshape(groups, 32, 128)
                low, high = swap_halves(part[:, :16], part[:, 16:])
                out_ref[c * 8 + tp + h, 0] = low.astype(BF16)
                out_ref[c * 8 + tp + h, 1] = high.astype(BF16)


def on_device(
    prior_sample, measured_position, measured_tally, measured_datum, measured_noise_spread
):
    part, level_count, width, line_total = prior_sample.shape
    groups, tiles = lax.axis_size("mem"), lax.axis_size("tile")
    members = groups * part
    cells = level_count * TILE_WIDTH
    slots = measured_position.shape[2]
    chunk = (line_total, 16, 128)
    paired = (tiles // 2, 2, groups, 16, 128)
    half = part * level_count * width // 2
    scratch = [
        pltpu.VMEM((PIECES, 2, half // PIECES, line_total), BF16),
        pltpu.VMEM((line_total * 16, 128), F32),
        pltpu.SemaphoreType.DMA((PIECES,)),
    ]
    places = np.arange(line_total)
    rows = [int(r) for r in row_of(places % tiles, places // tiles)]
    device = {r: d for d, r in enumerate(rows)}
    to_owner = [(r, device[r]) for r in range(line_total)]
    to_mate = [(device[r], device[r ^ 1]) for r in range(line_total)]
    to_far = [(device[r], device[r + 1]) for r in range(1, line_total - 1, 2)]
    to_far = to_far + [(b, a) for a, b in to_far]

    vmem = pl.BlockSpec(memory_space=pltpu.VMEM)
    anywhere = pl.BlockSpec(memory_space=pltpu.HBM)
    parted = call(
        split_kernel,
        jax.ShapeDtypeStruct(chunk, BF16),
        out_specs=anywhere,
        scratch=[pltpu.VMEM((PIECES, line_total // PIECES, 16, 128), BF16)] + scratch[1:],
    )(prior_sample.reshape(2, half, line_total))
    observed = call(
        pack_kernel,
        jax.ShapeDtypeStruct((8, slots), F32),
        in_specs=[vmem, vmem, vmem, pl.BlockSpec(memory_space=pltpu.SMEM)],
    )(measured_position[0], measured_datum[0], measured_noise_spread[0], measured_tally)
    observed = lax.ppermute(observed, MEM, to_owner)
    relaid = lax.all_to_all(parted, TILE_FIRST, split_axis=0, concat_axis=0, tiled=True)
    row_cells, packed = call(
        observe_kernel,
        (
            jax.ShapeDtypeStruct((2, members, cells), BF16),
            jax.ShapeDtypeStruct((2, members + 16, slots), BF16),
        ),
    )(relaid.reshape(paired), observed)
    far = lax.ppermute(packed, MEM, to_far)
    system, force, hand = call(
        gram_kernel,
        (
            jax.ShapeDtypeStruct((2, members, members), F32),
            jax.ShapeDtypeStruct((2, 1, members), F32),
            jax.ShapeDtypeStruct(packed.shape, BF16),
        ),
    )(packed)
    mate = lax.ppermute(hand, MEM, to_mate)
    anomaly, average, force = call(
        anomaly_kernel,
        (
            jax.ShapeDtypeStruct((2, members, cells), BF16),
            jax.ShapeDtypeStruct((2, 1, cells), F32),
            jax.ShapeDtypeStruct(force.shape, F32),
        ),
    )(row_cells, force)
    analyzed = call(
        update_kernel,
        jax.ShapeDtypeStruct(paired, BF16),
    )(system, force, mate, far, anomaly, average)
    returned = lax.all_to_all(
        analyzed.reshape(chunk), TILE_FIRST, split_axis=0, concat_axis=0, tiled=True
    )
    merged = call(
        merge_kernel,
        jax.ShapeDtypeStruct((2, half, line_total), BF16),
        out_specs=anywhere,
        scratch=scratch,
    )(returned)
    return merged.reshape(part, level_count, width, line_total)


def solution(mesh):
    placed = (
        P("mem", None, "tile", None),
        P(MEM, None, None),
        P(MEM, None),
        P(MEM, None, None),
        P(MEM, None, None),
    )
    return jax.shard_map(
        on_device,
        mesh=mesh,
        in_specs=placed,
        out_specs=P("mem", None, "tile", None),
        check_vma=False,
    )
```

```python
import math

import jax
import jax.numpy as jnp
import numpy as np
from jax import lax
from jax.experimental import pallas as pl
from jax.experimental.pallas import tpu as pltpu
from jax.sharding import PartitionSpec as P

TILE_WIDTH = 128
MEM = ("mem", "tile")
TILE_FIRST = ("tile", "mem")
VMEM_LIMIT = 48 * 1024 * 1024
F32 = jnp.float32
BF16 = jnp.bfloat16
NT = (((1,), (1,)), ((), ()))
NN = (((1,), (0,)), ((), ()))


def dot(a, b, dims=NN):
    return lax.dot_general(a, b, dims, preferred_element_type=F32)


def dot_full(a, b, dims=NN):
    return lax.dot_general(
        a, b, dims, precision=lax.Precision.HIGHEST, preferred_element_type=F32
    )


def call(body, out_shape, in_specs=None, out_specs=None, scratch=(), cost=None, limit=VMEM_LIMIT):
    extra = {} if in_specs is None else {"in_specs": in_specs}
    if out_specs is not None:
        extra["out_specs"] = out_specs
    return pl.pallas_call(
        body,
        out_shape=out_shape,
        scratch_shapes=scratch,
        cost_estimate=cost,
        compiler_params=pltpu.CompilerParams(vmem_limit_bytes=limit),
        **extra,
    )


def eye(rows, cols, shift=0):
    down = lax.broadcasted_iota(jnp.int32, (rows, cols), 0)
    along = lax.broadcasted_iota(jnp.int32, (rows, cols), 1)
    return jnp.where(along == down + shift, 1.0, 0.0).astype(F32)


def row_of(tile, mem):
    x, core, z, y = mem >> 1, mem & 1, tile >> 2, tile & 3
    along_y = y + (x & 1) * (3 - 2 * y)
    along_z = z + (along_y & 1) * (7 - 2 * z)
    return 2 * (x * 32 + along_y * 8 + along_z) + core


def row_of_chunk(chunk):
    return row_of(chunk >> 3, chunk & 7)


PIECES = 8


def split_kernel(x_ref, out_ref, held_ref, wide_ref, sems):
    rows = x_ref.shape[2]
    span = rows // PIECES
    owned = row_of_chunk(lax.broadcasted_iota(jnp.int32, (rows, 128), 0))
    along = lax.broadcasted_iota(jnp.int32, (rows, 128), 1)
    choice = jnp.concatenate(
        [jnp.where(owned == along + r, 1.0, 0.0) for r in range(0, rows, 128)], axis=1
    ).astype(BF16)
    for g in range(0, 16, 2):
        both = [
            x_ref[:, h * 64 : (h + 1) * 64, :].reshape(128, rows) for h in (g, g + 1)
        ]
        both = dot(choice, jnp.concatenate(both, axis=0), NT)
        wide_ref[pl.ds(g, rows, stride=16), :] = both[:, :128]
        wide_ref[pl.ds(g + 1, rows, stride=16), :] = both[:, 128:]
    copies = []
    for i in range(PIECES):
        d = i * span
        held_ref[i] = wide_ref[d * 16 : (d + span) * 16, :].astype(BF16).reshape(span, 16, 128)
        copy = pltpu.make_async_copy(held_ref.at[i], out_ref.at[pl.ds(d, span)], sems.at[i])
        copy.start()
        copies.append(copy)
    for copy in copies:
        copy.wait()


def pack_kernel(pos_ref, datum_ref, noise_ref, tally_ref, obs_ref):
    slots = pos_ref.shape[1]
    pos = pos_ref[...]
    level, col = pos >> 7, pos & 127
    obs_ref[0:2, :] = (((col >> 3) << 6) + (level << 3) + (col & 7)).astype(F32)
    obs_ref[2:4, :] = datum_ref[...]
    slot = lax.broadcasted_iota(jnp.int32, (1, slots), 1)
    for c in range(2):
        weights = 1.0 / noise_ref[c : c + 1, :].astype(F32)
        obs_ref[4 + c : 5 + c, :] = jnp.where(slot < tally_ref[0, c], weights, 0.0)
    obs_ref[6:8, :] = jnp.zeros((2, slots), F32)


def merge_kernel(x_ref, out_ref, held_ref, wide_ref, sems):
    rows = x_ref.shape[0]
    span = out_ref.shape[1] // PIECES
    for chunk in range(rows):
        r = row_of_chunk(chunk)
        wide_ref[r * 16 : (r + 1) * 16, :] = x_ref[chunk].astype(F32)
    unit = eye(128, 128).astype(BF16)
    copies = []
    for i in range(PIECES):
        for h in range(span // 64):
            g = i * (span // 64) + h
            part = wide_ref[pl.ds(g, rows, stride=16), :].astype(BF16)
            turned = dot(unit, part, NT).astype(BF16)
            held_ref[i, :, h * 64 : (h + 1) * 64, :] = turned.reshape(2, 64, rows)
        copy = pltpu.make_async_copy(
            held_ref.at[i], out_ref.at[:, pl.ds(i * span, span), :], sems.at[i]
        )
        copy.start()
        copies.append(copy)
    for copy in copies:
        copy.wait()


def swap_halves(low, high):
    left = lax.broadcasted_iota(jnp.int32, low.shape, low.ndim - 1) < 64
    axis = low.ndim - 1
    inner = pltpu.roll(jnp.where(left, high, low), 64, axis)
    return jnp.where(left, low, inner), jnp.where(left, inner, high)


def observe_kernel(x_ref, obs_ref, cells_ref, pack_ref):
    members = cells_ref.shape[1]
    cell_total = cells_ref.shape[2]
    slots = pack_ref.shape[2]
    for c in range(2):
        for tp in range(8):
            first, second = swap_halves(x_ref[c * 8 + tp, 0], x_ref[c * 8 + tp, 1])
            cells = jnp.concatenate([first, second], axis=1).reshape(members, 128)
            cells_ref[c, :, tp * 128 : (tp + 1) * 128] = cells
        place = obs_ref[c : c + 1, :].astype(jnp.int32)
        chosen = lax.broadcasted_iota(jnp.int32, (cell_total, slots), 0) == place
        chosen = jnp.where(chosen, 1.0, 0.0).astype(BF16)
        found = dot(cells_ref[c], chosen)
        average = jnp.sum(found, axis=0, keepdims=True) / members
        pack_ref[c, :members, :] = (found - average).astype(BF16)
        innovation = obs_ref[2 + c : 3 + c, :] - average
        weights = obs_ref[4 + c : 5 + c, :]
        sub = lax.broadcasted_iota(jnp.int32, (16, slots), 0)
        tail = jnp.where(sub == 0, innovation, jnp.where(sub == 1, weights, 0.0))
        pack_ref[c, members:, :] = tail.astype(BF16)


def invert64(rows):
    shape = rows[0].shape
    sub = lax.broadcasted_iota(jnp.int32, shape, 0)
    lane = lax.broadcasted_iota(jnp.int32, shape, 1)
    half, own = lane & 64, lane & 63
    unit = jnp.where((lane & 7) == sub, 1.0, 0.0)

    def spread(x, col):
        return jnp.take_along_axis(x, half + col, axis=1)

    def sublane(x, i):
        return jnp.broadcast_to(x[i : i + 1, :], shape)

    rows = list(rows)
    following = [spread(rows[0], j) for j in range(8)]
    for b in range(8):
        cols = {(b, j): following[j] for j in range(8)}
        following = []
        for i in range(b + 1, 8):
            for j in range(8):
                cols[i, j] = spread(rows[i], 8 * b + j)
            if i == b + 1:
                following = [spread(rows[i], 8 * i + j) for j in range(8)]
        here = (own >> 3) == b
        for i in range(b, 8):
            rows[i] = jnp.where(here, unit if i == b else 0.0, rows[i])
        pivots = None
        for r in range(8):
            pivot = sublane(cols[b, r], r)
            pivots = pivot if r == 0 else jnp.where(sub == r, pivot, pivots)
            inverse = 1.0 / pivot
            factors = {}
            for i in range(b, 8):
                factor = cols[i, r] * inverse
                factors[i] = jnp.where(sub > r, factor, 0.0) if i == b else factor
            following = [
                f - factors[b + 1] * sublane(cols[b + 1, r], j) for j, f in enumerate(following)
            ]
            for j in range(r + 1, 8):
                head = sublane(cols[b, j], r)
                cols[b, j] = cols[b, j] - (cols[b, r] * head) * inverse
                for i in range(b + 1, 8):
                    cols[i, j] = cols[i, j] - factors[i] * head
            row = sublane(rows[b], r)
            for i in range(b, 8):
                if i > b or r < 7:
                    rows[i] = rows[i] - factors[i] * row
        rows[b] = jnp.where(own <= sub + 8 * b, rows[b] * lax.rsqrt(pivots), 0.0)
    return rows


def invert256(systems, low, high):
    left = lax.broadcasted_iota(jnp.int32, (64, 128), 1) < 64
    unit_right = eye(64, 128, 64)

    def turn(x):
        return pltpu.roll(x, 64, 1)

    def run(low, high):
        both = jnp.where(left, low, high)
        done = jnp.concatenate(invert64([both[8 * i : 8 * i + 8] for i in range(8)]), axis=0)
        return jnp.where(left, done, 0.0), jnp.where(left, 0.0, done)

    def times(t, half, x):
        if half:
            return dot_full(t, jnp.concatenate([jnp.zeros(x.shape, F32), x], axis=0))
        return dot_full(t[:, :64], x)

    def times_t(x, t, half):
        return dot_full(x, t, NT) if half else dot_full(x[:, :64], t[:, :64], NT)

    two = range(2)
    near = [s[:, :128] for s in systems]
    turned = [turn(x) for x in near]
    swapped = [turned[0], near[1]]
    facing = [near[0], turned[1]]

    t0 = run(low, high)
    u0 = [times(t0[c], c, swapped[c][:64]) for c in two]
    m0 = [times_t(facing[c][64:128], t0[c], c) for c in two]
    s1 = [swapped[c][64:128] - dot_full(m0[c], u0[c]) for c in two]

    t1 = run(*s1)
    v0 = [times(t0[c], c, systems[c][:64, 128:]) for c in two]
    n0 = [times_t(facing[c][128:], t0[c], c) for c in two]
    up1 = [systems[c][64:128, 128:] - dot_full(m0[c], v0[c]) for c in two]
    down1 = [swapped[c][128:] - dot_full(n0[c], u0[c]) for c in two]
    rest = [systems[c][128:, 128:] - dot_full(n0[c], v0[c]) for c in two]
    up1, rest = [up1[0], turn(up1[1])], [rest[0], turn(rest[1])]
    u1 = [times(t1[c], c, up1[c]) for c in two]
    m1 = [times_t(down1[c], t1[c], c) for c in two]
    s2 = [rest[c][:64] - dot_full(m1[c][:64], u1[c]) for c in two]

    t2 = run(*s2)
    low2 = [rest[c][64:] - dot_full(m1[c][64:], u1[c]) for c in two]
    l0 = [t0[0], turn(t0[1])]
    l1 = [
        times(t1[c], c, jnp.where(left, -dot_full(m0[c], l0[c]), unit_right)) for c in two
    ]
    r2 = [dot_full(n0[c], l0[c]) + dot_full(m1[c], l1[c]) for c in two]
    u2 = [times(t2[c], c, s2[c]) for c in two]
    m2 = [times_t(low2[c], t2[c], c) for c in two]
    s3 = [low2[c] - dot_full(m2[c], u2[c]) for c in two]

    t3 = run(s3[1], s3[0])[::-1]
    third = [t2[0], turn(t2[1])]
    l2 = [-times(t2[c], c, r2[c][:64]) for c in two]
    r3 = [r2[c][64:] + dot_full(m2[c], l2[c]) for c in two]
    r3_right = [jnp.where(left, -dot_full(m2[c], third[c]), unit_right) for c in two]
    rows = []
    for c in two:
        last = times(t3[c], 1 - c, jnp.concatenate([-r3[c], r3_right[c]], axis=1))
        rows.append([l0[c], l1[c], jnp.concatenate([l2[c], third[c]], axis=1), last])
    return rows


def observed_block(refs, c, members):
    ens, wtd, inn = [], [], []
    for ref in refs:
        ensemble = ref[c, :members, :]
        tail = ref[c, members:, :]
        weights = tail[1:2, :].astype(F32)
        ens.append(ensemble)
        wtd.append((weights * ensemble.astype(F32)).astype(BF16))
        inn.append(tail)
    if len(refs) > 1:
        return tuple(jnp.concatenate(p, axis=1) for p in (ens, wtd, inn))
    return ens[0], wtd[0], inn[0]


def tapered(blocks, falloff, rows, spans):
    def pick(x):
        return jnp.concatenate([x[at] for at in spans], axis=0) if len(spans) > 1 else x[spans[0]]

    grams = [
        0.5 * falloff * (dot(wtd[rows], pick(ens), NT) + dot(ens[rows], pick(wtd), NT))
        for ens, wtd, _ in blocks
    ]
    return [grams[c] + 0.5 * grams[1 - c] for c in range(2)]


def tapered_forcing(blocks, falloff):
    forces = [falloff * dot(inn, wtd, NT)[0:1] for _, wtd, inn in blocks]
    return [forces[c] + 0.5 * forces[1 - c] for c in range(2)]


def gram_kernel(own_ref, system_ref, force_ref, hand_ref):
    members = system_ref.shape[1]
    hand_ref[...] = own_ref[...]
    blocks = [observed_block([own_ref], c, members) for c in range(2)]
    grams = tapered(blocks, 1.0, slice(0, members), [slice(0, members)])
    forces = tapered_forcing(blocks, 1.0)
    spread = (members - 1) * eye(members, members)
    for c in range(2):
        system_ref[c] = spread + grams[c]
        force_ref[c] = forces[c]


def anomaly_kernel(cells_ref, force_ref, anom_ref, avg_ref, same_ref):
    members = cells_ref.shape[1]
    same_ref[...] = force_ref[...]
    for c in range(2):
        for at in range(0, cells_ref.shape[2], 128):
            cells = cells_ref[c, :, at : at + 128].astype(F32)
            average = jnp.sum(cells, axis=0, keepdims=True) / members
            anom_ref[c, :, at : at + 128] = (cells - average).astype(BF16)
            avg_ref[c, :, at : at + 128] = average


def update_kernel(system_ref, force_ref, mate_ref, far_ref, anom_ref, avg_ref, out_ref):
    members = anom_ref.shape[1]
    groups = members // 32
    blocks = [observed_block([mate_ref, far_ref], c, members) for c in range(2)]
    head, whole = slice(0, 64), slice(0, members)
    low = tapered(blocks, 0.5, head, [slice(0, 128)])[0]
    high = tapered(blocks, 0.5, head, [slice(64, 128), slice(0, 64)])[1]
    low = system_ref[0, :64, :128] + low
    high = pltpu.roll(system_ref[1, :64, :128], 64, 1) + high
    grams = tapered(blocks, 0.5, whole, [whole])
    systems = [system_ref[c] + grams[c] for c in range(2)]
    forces = tapered_forcing(blocks, 0.5)
    forces = [force_ref[c] + forces[c] for c in range(2)]
    inverses = invert256(systems, low, high)
    for c in range(2):
        force = forces[c]
        mean_weight = jnp.zeros((1, members), F32)
        for rows in inverses[c]:
            if rows.shape[1] < members:
                halfway = jnp.sum(rows * force[:, :128], axis=1, keepdims=True)
                part = jnp.sum(rows * halfway, axis=0, keepdims=True)
                part = jnp.concatenate([part, jnp.zeros((1, 128), F32)], axis=1)
            else:
                halfway = jnp.sum(rows * force, axis=1, keepdims=True)
                part = jnp.sum(rows * halfway, axis=0, keepdims=True)
            mean_weight = mean_weight + part
        scale = math.sqrt(members - 1)
        mixing = []
        for rows in inverses[c]:
            if rows.shape[1] < members:
                rows = jnp.concatenate([rows, jnp.zeros((64, 128), F32)], axis=1)
            mixing.append((scale * rows + mean_weight).astype(BF16))
        mixing = jnp.concatenate(mixing, axis=0)
        for tp in range(0, 8, 2):
            span = slice(tp * 128, (tp + 2) * 128)
            made = dot(mixing, anom_ref[c, :, span]) + avg_ref[c, :, span]
            for h in range(2):
                part = made[:, h * 128 : (h + 1) * 128].reshape(groups, 32, 128)
                low, high = swap_halves(part[:, :16], part[:, 16:])
                out_ref[c * 8 + tp + h, 0] = low.astype(BF16)
                out_ref[c * 8 + tp + h, 1] = high.astype(BF16)


def on_device(
    prior_sample, measured_position, measured_tally, measured_datum, measured_noise_spread
):
    part, level_count, width, line_total = prior_sample.shape
    groups, tiles = lax.axis_size("mem"), lax.axis_size("tile")
    members = groups * part
    cells = level_count * TILE_WIDTH
    slots = measured_position.shape[2]
    chunk = (line_total, 16, 128)
    paired = (tiles // 2, 2, groups, 16, 128)
    half = part * level_count * width // 2
    scratch = [
        pltpu.VMEM((PIECES, 2, half // PIECES, line_total), BF16),
        pltpu.VMEM((line_total * 16 + 128, 128), F32),
        pltpu.SemaphoreType.DMA((PIECES,)),
    ]
    places = np.arange(line_total)
    rows = [int(r) for r in row_of(places % tiles, places // tiles)]
    device = {r: d for d, r in enumerate(rows)}
    to_owner = [(r, device[r]) for r in range(line_total)]
    to_mate = [(device[r], device[r ^ 1]) for r in range(line_total)]
    to_far = [(device[r], device[r + 1]) for r in range(1, line_total - 1, 2)]
    to_far = to_far + [(b, a) for a, b in to_far]

    vmem = pl.BlockSpec(memory_space=pltpu.VMEM)
    anywhere = pl.BlockSpec(memory_space=pltpu.HBM)
    parted = call(
        split_kernel,
        jax.ShapeDtypeStruct(chunk, BF16),
        out_specs=anywhere,
        scratch=[pltpu.VMEM((PIECES, line_total // PIECES, 16, 128), BF16)] + scratch[1:],
    )(prior_sample.reshape(2, half, line_total))
    observed = call(
        pack_kernel,
        jax.ShapeDtypeStruct((8, slots), F32),
        in_specs=[vmem, vmem, vmem, pl.BlockSpec(memory_space=pltpu.SMEM)],
    )(measured_position[0], measured_datum[0], measured_noise_spread[0], measured_tally)
    observed = lax.ppermute(observed, MEM, to_owner)
    relaid = lax.all_to_all(parted, TILE_FIRST, split_axis=0, concat_axis=0, tiled=True)
    row_cells, packed = call(
        observe_kernel,
        (
            jax.ShapeDtypeStruct((2, members, cells), BF16),
            jax.ShapeDtypeStruct((2, members + 16, slots), BF16),
        ),
    )(relaid.reshape(paired), observed)
    far = lax.ppermute(packed, MEM, to_far)
    system, force, hand = call(
        gram_kernel,
        (
            jax.ShapeDtypeStruct((2, members, members), F32),
            jax.ShapeDtypeStruct((2, 1, members), F32),
            jax.ShapeDtypeStruct(packed.shape, BF16),
        ),
    )(packed)
    mate = lax.ppermute(hand, MEM, to_mate)
    anomaly, average, force = call(
        anomaly_kernel,
        (
            jax.ShapeDtypeStruct((2, members, cells), BF16),
            jax.ShapeDtypeStruct((2, 1, cells), F32),
            jax.ShapeDtypeStruct(force.shape, F32),
        ),
    )(row_cells, force)
    analyzed = call(
        update_kernel,
        jax.ShapeDtypeStruct(paired, BF16),
    )(system, force, mate, far, anomaly, average)
    returned = lax.all_to_all(
        analyzed.reshape(chunk), TILE_FIRST, split_axis=0, concat_axis=0, tiled=True
    )
    merged = call(
        merge_kernel,
        jax.ShapeDtypeStruct((2, half, line_total), BF16),
        out_specs=anywhere,
        scratch=scratch,
    )(returned)
    return merged.reshape(part, level_count, width, line_total)


def solution(mesh):
    placed = (
        P("mem", None, "tile", None),
        P(MEM, None, None),
        P(MEM, None),
        P(MEM, None, None),
        P(MEM, None, None),
    )
    return jax.shard_map(
        on_device,
        mesh=mesh,
        in_specs=placed,
        out_specs=P("mem", None, "tile", None),
        check_vma=False,
    )
```

```python
import math

import jax
import jax.numpy as jnp
import numpy as np
from jax import lax
from jax.experimental import pallas as pl
from jax.experimental.pallas import tpu as pltpu
from jax.sharding import PartitionSpec as P

TILE_WIDTH = 128
MEM = ("mem", "tile")
TILE_FIRST = ("tile", "mem")
VMEM_LIMIT = 48 * 1024 * 1024
F32 = jnp.float32
BF16 = jnp.bfloat16
NT = (((1,), (1,)), ((), ()))
NN = (((1,), (0,)), ((), ()))


def dot(a, b, dims=NN):
    return lax.dot_general(a, b, dims, preferred_element_type=F32)


def dot_full(a, b, dims=NN):
    return lax.dot_general(
        a, b, dims, precision=lax.Precision.HIGHEST, preferred_element_type=F32
    )


def call(body, out_shape, in_specs=None, out_specs=None, scratch=(), cost=None, limit=VMEM_LIMIT):
    extra = {} if in_specs is None else {"in_specs": in_specs}
    if out_specs is not None:
        extra["out_specs"] = out_specs
    return pl.pallas_call(
        body,
        out_shape=out_shape,
        scratch_shapes=scratch,
        cost_estimate=cost,
        compiler_params=pltpu.CompilerParams(vmem_limit_bytes=limit),
        **extra,
    )


def eye(rows, cols, shift=0):
    down = lax.broadcasted_iota(jnp.int32, (rows, cols), 0)
    along = lax.broadcasted_iota(jnp.int32, (rows, cols), 1)
    return jnp.where(along == down + shift, 1.0, 0.0).astype(F32)


def row_of(tile, mem):
    x, core, z, y = mem >> 1, mem & 1, tile >> 2, tile & 3
    along_y = y + (z & 1) * (3 - 2 * y)
    along_x = x + (along_y & 1) * (3 - 2 * x)
    return 2 * (z * 16 + along_y * 4 + along_x) + core


def row_of_chunk(chunk):
    return row_of(chunk >> 3, chunk & 7)


PIECES = 8


def split_kernel(x_ref, out_ref, held_ref, wide_ref, sems):
    rows = x_ref.shape[2]
    span = rows // PIECES
    owned = row_of_chunk(lax.broadcasted_iota(jnp.int32, (rows, 128), 0))
    along = lax.broadcasted_iota(jnp.int32, (rows, 128), 1)
    choice = jnp.concatenate(
        [jnp.where(owned == along + r, 1.0, 0.0) for r in range(0, rows, 128)], axis=1
    ).astype(BF16)
    for g in range(0, 16, 2):
        both = [
            x_ref[:, h * 64 : (h + 1) * 64, :].reshape(128, rows) for h in (g, g + 1)
        ]
        both = dot(choice, jnp.concatenate(both, axis=0), NT)
        wide_ref[pl.ds(g, rows, stride=16), :] = both[:, :128]
        wide_ref[pl.ds(g + 1, rows, stride=16), :] = both[:, 128:]
    copies = []
    for i in range(PIECES):
        d = i * span
        held_ref[i] = wide_ref[d * 16 : (d + span) * 16, :].astype(BF16).reshape(span, 16, 128)
        copy = pltpu.make_async_copy(held_ref.at[i], out_ref.at[pl.ds(d, span)], sems.at[i])
        copy.start()
        copies.append(copy)
    for copy in copies:
        copy.wait()


def pack_kernel(pos_ref, datum_ref, noise_ref, tally_ref, obs_ref):
    slots = pos_ref.shape[1]
    pos = pos_ref[...]
    level, col = pos >> 7, pos & 127
    obs_ref[0:2, :] = (((col >> 3) << 6) + (level << 3) + (col & 7)).astype(F32)
    obs_ref[2:4, :] = datum_ref[...]
    slot = lax.broadcasted_iota(jnp.int32, (1, slots), 1)
    for c in range(2):
        weights = 1.0 / noise_ref[c : c + 1, :].astype(F32)
        obs_ref[4 + c : 5 + c, :] = jnp.where(slot < tally_ref[0, c], weights, 0.0)
    obs_ref[6:8, :] = jnp.zeros((2, slots), F32)


def merge_kernel(x_ref, out_ref, held_ref, wide_ref, sems):
    rows = x_ref.shape[0]
    span = out_ref.shape[1] // PIECES
    for chunk in range(rows):
        r = row_of_chunk(chunk)
        wide_ref[r * 16 : (r + 1) * 16, :] = x_ref[chunk].astype(F32)
    unit = eye(128, 128).astype(BF16)
    copies = []
    for i in range(PIECES):
        for h in range(span // 64):
            g = i * (span // 64) + h
            part = wide_ref[pl.ds(g, rows, stride=16), :].astype(BF16)
            turned = dot(unit, part, NT).astype(BF16)
            held_ref[i, :, h * 64 : (h + 1) * 64, :] = turned.reshape(2, 64, rows)
        copy = pltpu.make_async_copy(
            held_ref.at[i], out_ref.at[:, pl.ds(i * span, span), :], sems.at[i]
        )
        copy.start()
        copies.append(copy)
    for copy in copies:
        copy.wait()


def swap_halves(low, high):
    left = lax.broadcasted_iota(jnp.int32, low.shape, low.ndim - 1) < 64
    axis = low.ndim - 1
    inner = pltpu.roll(jnp.where(left, high, low), 64, axis)
    return jnp.where(left, low, inner), jnp.where(left, inner, high)


def observe_kernel(x_ref, obs_ref, cells_ref, pack_ref):
    members = cells_ref.shape[1]
    cell_total = cells_ref.shape[2]
    slots = pack_ref.shape[2]
    for c in range(2):
        for tp in range(8):
            first, second = swap_halves(x_ref[c * 8 + tp, 0], x_ref[c * 8 + tp, 1])
            cells = jnp.concatenate([first, second], axis=1).reshape(members, 128)
            cells_ref[c, :, tp * 128 : (tp + 1) * 128] = cells
        place = obs_ref[c : c + 1, :].astype(jnp.int32)
        chosen = lax.broadcasted_iota(jnp.int32, (cell_total, slots), 0) == place
        chosen = jnp.where(chosen, 1.0, 0.0).astype(BF16)
        found = dot(cells_ref[c], chosen)
        average = jnp.sum(found, axis=0, keepdims=True) / members
        pack_ref[c, :members, :] = (found - average).astype(BF16)
        innovation = obs_ref[2 + c : 3 + c, :] - average
        weights = obs_ref[4 + c : 5 + c, :]
        sub = lax.broadcasted_iota(jnp.int32, (16, slots), 0)
        tail = jnp.where(sub == 0, innovation, jnp.where(sub == 1, weights, 0.0))
        pack_ref[c, members:, :] = tail.astype(BF16)


def invert64(rows):
    shape = rows[0].shape
    sub = lax.broadcasted_iota(jnp.int32, shape, 0)
    lane = lax.broadcasted_iota(jnp.int32, shape, 1)
    half, own = lane & 64, lane & 63
    unit = jnp.where((lane & 7) == sub, 1.0, 0.0)

    def spread(x, col):
        return jnp.take_along_axis(x, half + col, axis=1)

    def sublane(x, i):
        return jnp.broadcast_to(x[i : i + 1, :], shape)

    rows = list(rows)
    following = [spread(rows[0], j) for j in range(8)]
    for b in range(8):
        cols = {(b, j): following[j] for j in range(8)}
        following = []
        for i in range(b + 1, 8):
            for j in range(8):
                cols[i, j] = spread(rows[i], 8 * b + j)
            if i == b + 1:
                following = [spread(rows[i], 8 * i + j) for j in range(8)]
        here = (own >> 3) == b
        for i in range(b, 8):
            rows[i] = jnp.where(here, unit if i == b else 0.0, rows[i])
        pivots = None
        for r in range(8):
            pivot = sublane(cols[b, r], r)
            pivots = pivot if r == 0 else jnp.where(sub == r, pivot, pivots)
            inverse = 1.0 / pivot
            factors = {}
            for i in range(b, 8):
                factor = cols[i, r] * inverse
                factors[i] = jnp.where(sub > r, factor, 0.0) if i == b else factor
            following = [
                f - factors[b + 1] * sublane(cols[b + 1, r], j) for j, f in enumerate(following)
            ]
            for j in range(r + 1, 8):
                head = sublane(cols[b, j], r)
                cols[b, j] = cols[b, j] - (cols[b, r] * head) * inverse
                for i in range(b + 1, 8):
                    cols[i, j] = cols[i, j] - factors[i] * head
            row = sublane(rows[b], r)
            for i in range(b, 8):
                if i > b or r < 7:
                    rows[i] = rows[i] - factors[i] * row
        rows[b] = jnp.where(own <= sub + 8 * b, rows[b] * lax.rsqrt(pivots), 0.0)
    return rows


def invert256(systems, low, high):
    left = lax.broadcasted_iota(jnp.int32, (64, 128), 1) < 64
    unit_right = eye(64, 128, 64)

    def turn(x):
        return pltpu.roll(x, 64, 1)

    def run(low, high):
        both = jnp.where(left, low, high)
        done = jnp.concatenate(invert64([both[8 * i : 8 * i + 8] for i in range(8)]), axis=0)
        return jnp.where(left, done, 0.0), jnp.where(left, 0.0, done)

    def times(t, half, x):
        if half:
            return dot_full(t, jnp.concatenate([jnp.zeros(x.shape, F32), x], axis=0))
        return dot_full(t[:, :64], x)

    def times_t(x, t, half):
        return dot_full(x, t, NT) if half else dot_full(x[:, :64], t[:, :64], NT)

    two = range(2)
    near = [s[:, :128] for s in systems]
    turned = [turn(x) for x in near]
    swapped = [turned[0], near[1]]
    facing = [near[0], turned[1]]

    t0 = run(low, high)
    u0 = [times(t0[c], c, swapped[c][:64]) for c in two]
    m0 = [times_t(facing[c][64:128], t0[c], c) for c in two]
    s1 = [swapped[c][64:128] - dot_full(m0[c], u0[c]) for c in two]

    t1 = run(*s1)
    v0 = [times(t0[c], c, systems[c][:64, 128:]) for c in two]
    n0 = [times_t(facing[c][128:], t0[c], c) for c in two]
    up1 = [systems[c][64:128, 128:] - dot_full(m0[c], v0[c]) for c in two]
    down1 = [swapped[c][128:] - dot_full(n0[c], u0[c]) for c in two]
    rest = [systems[c][128:, 128:] - dot_full(n0[c], v0[c]) for c in two]
    up1, rest = [up1[0], turn(up1[1])], [rest[0], turn(rest[1])]
    u1 = [times(t1[c], c, up1[c]) for c in two]
    m1 = [times_t(down1[c], t1[c], c) for c in two]
    s2 = [rest[c][:64] - dot_full(m1[c][:64], u1[c]) for c in two]

    t2 = run(*s2)
    low2 = [rest[c][64:] - dot_full(m1[c][64:], u1[c]) for c in two]
    l0 = [t0[0], turn(t0[1])]
    l1 = [
        times(t1[c], c, jnp.where(left, -dot_full(m0[c], l0[c]), unit_right)) for c in two
    ]
    r2 = [dot_full(n0[c], l0[c]) + dot_full(m1[c], l1[c]) for c in two]
    u2 = [times(t2[c], c, s2[c]) for c in two]
    m2 = [times_t(low2[c], t2[c], c) for c in two]
    s3 = [low2[c] - dot_full(m2[c], u2[c]) for c in two]

    t3 = run(s3[1], s3[0])[::-1]
    third = [t2[0], turn(t2[1])]
    l2 = [-times(t2[c], c, r2[c][:64]) for c in two]
    r3 = [r2[c][64:] + dot_full(m2[c], l2[c]) for c in two]
    r3_right = [jnp.where(left, -dot_full(m2[c], third[c]), unit_right) for c in two]
    rows = []
    for c in two:
        last = times(t3[c], 1 - c, jnp.concatenate([-r3[c], r3_right[c]], axis=1))
        rows.append([l0[c], l1[c], jnp.concatenate([l2[c], third[c]], axis=1), last])
    return rows


def observed_block(refs, c, members):
    ens, wtd, inn = [], [], []
    for ref in refs:
        ensemble = ref[c, :members, :]
        tail = ref[c, members:, :]
        weights = tail[1:2, :].astype(F32)
        ens.append(ensemble)
        wtd.append((weights * ensemble.astype(F32)).astype(BF16))
        inn.append(tail)
    if len(refs) > 1:
        return tuple(jnp.concatenate(p, axis=1) for p in (ens, wtd, inn))
    return ens[0], wtd[0], inn[0]


def tapered(blocks, falloff, rows, spans):
    def pick(x):
        return jnp.concatenate([x[at] for at in spans], axis=0) if len(spans) > 1 else x[spans[0]]

    grams = [
        0.5 * falloff * (dot(wtd[rows], pick(ens), NT) + dot(ens[rows], pick(wtd), NT))
        for ens, wtd, _ in blocks
    ]
    return [grams[c] + 0.5 * grams[1 - c] for c in range(2)]


def tapered_forcing(blocks, falloff):
    forces = [falloff * dot(inn, wtd, NT)[0:1] for _, wtd, inn in blocks]
    return [forces[c] + 0.5 * forces[1 - c] for c in range(2)]


def gram_kernel(own_ref, system_ref, force_ref, hand_ref):
    members = system_ref.shape[1]
    hand_ref[...] = own_ref[...]
    blocks = [observed_block([own_ref], c, members) for c in range(2)]
    grams = tapered(blocks, 1.0, slice(0, members), [slice(0, members)])
    forces = tapered_forcing(blocks, 1.0)
    spread = (members - 1) * eye(members, members)
    for c in range(2):
        system_ref[c] = spread + grams[c]
        force_ref[c] = forces[c]


def anomaly_kernel(cells_ref, force_ref, anom_ref, avg_ref, same_ref):
    members = cells_ref.shape[1]
    same_ref[...] = force_ref[...]
    for c in range(2):
        for at in range(0, cells_ref.shape[2], 128):
            cells = cells_ref[c, :, at : at + 128].astype(F32)
            average = jnp.sum(cells, axis=0, keepdims=True) / members
            anom_ref[c, :, at : at + 128] = (cells - average).astype(BF16)
            avg_ref[c, :, at : at + 128] = average


def update_kernel(system_ref, force_ref, mate_ref, far_ref, anom_ref, avg_ref, out_ref):
    members = anom_ref.shape[1]
    groups = members // 32
    blocks = [observed_block([mate_ref, far_ref], c, members) for c in range(2)]
    head, whole = slice(0, 64), slice(0, members)
    low = tapered(blocks, 0.5, head, [slice(0, 128)])[0]
    high = tapered(blocks, 0.5, head, [slice(64, 128), slice(0, 64)])[1]
    low = system_ref[0, :64, :128] + low
    high = pltpu.roll(system_ref[1, :64, :128], 64, 1) + high
    grams = tapered(blocks, 0.5, whole, [whole])
    systems = [system_ref[c] + grams[c] for c in range(2)]
    forces = tapered_forcing(blocks, 0.5)
    forces = [force_ref[c] + forces[c] for c in range(2)]
    inverses = invert256(systems, low, high)
    for c in range(2):
        force = forces[c]
        mean_weight = jnp.zeros((1, members), F32)
        for rows in inverses[c]:
            if rows.shape[1] < members:
                halfway = jnp.sum(rows * force[:, :128], axis=1, keepdims=True)
                part = jnp.sum(rows * halfway, axis=0, keepdims=True)
                part = jnp.concatenate([part, jnp.zeros((1, 128), F32)], axis=1)
            else:
                halfway = jnp.sum(rows * force, axis=1, keepdims=True)
                part = jnp.sum(rows * halfway, axis=0, keepdims=True)
            mean_weight = mean_weight + part
        scale = math.sqrt(members - 1)
        mixing = []
        for rows in inverses[c]:
            if rows.shape[1] < members:
                rows = jnp.concatenate([rows, jnp.zeros((64, 128), F32)], axis=1)
            mixing.append((scale * rows + mean_weight).astype(BF16))
        mixing = jnp.concatenate(mixing, axis=0)
        for tp in range(0, 8, 2):
            span = slice(tp * 128, (tp + 2) * 128)
            made = dot(mixing, anom_ref[c, :, span]) + avg_ref[c, :, span]
            for h in range(2):
                part = made[:, h * 128 : (h + 1) * 128].reshape(groups, 32, 128)
                low, high = swap_halves(part[:, :16], part[:, 16:])
                out_ref[c * 8 + tp + h, 0] = low.astype(BF16)
                out_ref[c * 8 + tp + h, 1] = high.astype(BF16)


def on_device(
    prior_sample, measured_position, measured_tally, measured_datum, measured_noise_spread
):
    part, level_count, width, line_total = prior_sample.shape
    groups, tiles = lax.axis_size("mem"), lax.axis_size("tile")
    members = groups * part
    cells = level_count * TILE_WIDTH
    slots = measured_position.shape[2]
    chunk = (line_total, 16, 128)
    paired = (tiles // 2, 2, groups, 16, 128)
    half = part * level_count * width // 2
    scratch = [
        pltpu.VMEM((PIECES, 2, half // PIECES, line_total), BF16),
        pltpu.VMEM((line_total * 16 + 128, 128), F32),
        pltpu.SemaphoreType.DMA((PIECES,)),
    ]
    places = np.arange(line_total)
    rows = [int(r) for r in row_of(places % tiles, places // tiles)]
    device = {r: d for d, r in enumerate(rows)}
    to_owner = [(r, device[r]) for r in range(line_total)]
    to_mate = [(device[r], device[r ^ 1]) for r in range(line_total)]
    to_far = [(device[r], device[r + 1]) for r in range(1, line_total - 1, 2)]
    to_far = to_far + [(b, a) for a, b in to_far]

    vmem = pl.BlockSpec(memory_space=pltpu.VMEM)
    anywhere = pl.BlockSpec(memory_space=pltpu.HBM)
    parted = call(
        split_kernel,
        jax.ShapeDtypeStruct(chunk, BF16),
        out_specs=anywhere,
        scratch=[pltpu.VMEM((PIECES, line_total // PIECES, 16, 128), BF16)] + scratch[1:],
    )(prior_sample.reshape(2, half, line_total))
    observed = call(
        pack_kernel,
        jax.ShapeDtypeStruct((8, slots), F32),
        in_specs=[vmem, vmem, vmem, pl.BlockSpec(memory_space=pltpu.SMEM)],
    )(measured_position[0], measured_datum[0], measured_noise_spread[0], measured_tally)
    observed = lax.ppermute(observed, MEM, to_owner)
    relaid = lax.all_to_all(parted, TILE_FIRST, split_axis=0, concat_axis=0, tiled=True)
    row_cells, packed = call(
        observe_kernel,
        (
            jax.ShapeDtypeStruct((2, members, cells), BF16),
            jax.ShapeDtypeStruct((2, members + 16, slots), BF16),
        ),
    )(relaid.reshape(paired), observed)
    far = lax.ppermute(packed, MEM, to_far)
    system, force, hand = call(
        gram_kernel,
        (
            jax.ShapeDtypeStruct((2, members, members), F32),
            jax.ShapeDtypeStruct((2, 1, members), F32),
            jax.ShapeDtypeStruct(packed.shape, BF16),
        ),
    )(packed)
    mate = lax.ppermute(hand, MEM, to_mate)
    anomaly, average, force = call(
        anomaly_kernel,
        (
            jax.ShapeDtypeStruct((2, members, cells), BF16),
            jax.ShapeDtypeStruct((2, 1, cells), F32),
            jax.ShapeDtypeStruct(force.shape, F32),
        ),
    )(row_cells, force)
    analyzed = call(
        update_kernel,
        jax.ShapeDtypeStruct(paired, BF16),
    )(system, force, mate, far, anomaly, average)
    returned = lax.all_to_all(
        analyzed.reshape(chunk), TILE_FIRST, split_axis=0, concat_axis=0, tiled=True
    )
    merged = call(
        merge_kernel,
        jax.ShapeDtypeStruct((2, half, line_total), BF16),
        out_specs=anywhere,
        scratch=scratch,
    )(returned)
    return merged.reshape(part, level_count, width, line_total)


def solution(mesh):
    placed = (
        P("mem", None, "tile", None),
        P(MEM, None, None),
        P(MEM, None),
        P(MEM, None, None),
        P(MEM, None, None),
    )
    return jax.shard_map(
        on_device,
        mesh=mesh,
        in_specs=placed,
        out_specs=P("mem", None, "tile", None),
        check_vma=False,
    )
```
